32 devices in a mesh: dom: 8 (over y, x, core), band: 4 (over z).
Axes of the slice: x: 2, y: 2, z: 4, core: 2. Of those that a mesh axis runs over, the one named last changes fastest.
Arguments:
- states: float32 [1536, 1536], P('dom', 'band'), may hold values from -6 to 6
- inv_mass: float32 [1536], P('dom'), may hold values from 0.5 to 2
- cell_ham: float32 [40, 343, 343], P('dom'), as said below
- cell_nodes: int32 [40, 343], P('dom'), may hold values from 0 to 287, as said below
- send_up: int32 [384], P('dom'), may hold values from 0 to 191, as said below
- send_down: int32 [384], P('dom'), may hold values from 0 to 191, as said below
- owner: int32 [8], replicated, may hold values from 0 to 7, each once
- rotation_store: float32 [1536, 1536], P('dom'), may hold values from -0.15625 to 0.15625
Outputs:
- rotated: float32 [1536, 1536], P('dom', 'band')
The draws below stay inside these ranges and needn't reach their ends.
Inputs may be any that keep to these rules, and one draw needn't show every extreme that they name: `cell_ham`: each cell's matrix is symmetric. `cell_nodes`: each domain's cells name every one of its extended nodes at least once. `send_up`: the 48 entries of one domain are distinct. `send_down`: the 48 entries of one domain are distinct. `owner`: a permutation.
All inputs are finite; a program needn't handle non-finite values.
Results may differ from the reference program's by a relative error of at most 0.00007.
Values sent between devices are 32-bit elements; how exact they have to be, the bound alone decides.
No kernel may reach another device: no remote copies, remote signals or barrier semaphores. Data moves between devices by JAX's collectives and lax.ppermute only.
A program may use at most 64 MiB of HBM per device.

```python
import math
import jax
import jax.numpy as jnp
from jax import lax

STATES = 1536
CELL_NODES = 343
OWNED_NODES = 192
GHOST_NODES = 48
DOMAIN_CELLS = 5
DOMAINS = 8
ALL_NODES = 1536
ALL_GHOSTS = 384
ALL_CELLS = 40
PANEL_ROWS = 192
N_DOM = 8


def swap_entries(values, left_spot, right_spot):
    left_value = values[left_spot]
    right_value = values[right_spot]
    return values.at[left_spot].set(right_value).at[right_spot].set(left_value)


def interface_lists(key, salt):
    domains = ALL_GHOSTS // GHOST_NODES
    base_key = jax.random.fold_in(key, salt)
    domain_keys = jax.random.split(base_key, domains)
    spot_key = jax.random.fold_in(base_key, 7)
    perms = jax.vmap(lambda one_key: jax.random.permutation(one_key, OWNED_NODES))(domain_keys)
    high_spot = jax.random.randint(jax.random.fold_in(spot_key, 1), (), 0, GHOST_NODES)
    step_size = jax.random.randint(jax.random.fold_in(spot_key, 2), (), 0, GHOST_NODES - 1)
    low_spot = (high_spot + 1 + step_size) % GHOST_NODES
    leading = perms[0]
    leading = swap_entries(leading, jnp.argmax(leading == OWNED_NODES - 1), high_spot)
    leading = swap_entries(leading, jnp.argmax(leading == 0), low_spot)
    perms = perms.at[0].set(leading)
    return perms[:, :GHOST_NODES].reshape(-1).astype(jnp.int32)


def draw_send_up(key, part):
    return interface_lists(key, 11)


def draw_send_down(key, part):
    return interface_lists(key, 12)


def draw_cell_nodes(key, part):
    domains = ALL_CELLS // DOMAIN_CELLS
    extended = OWNED_NODES + 2 * GHOST_NODES
    slot_count = DOMAIN_CELLS * CELL_NODES
    copies = -(-slot_count // extended)

    def one_domain(domain_key):
        pieces_list = [jax.random.permutation(jax.random.fold_in(domain_key, copy_index), extended) for copy_index in range(copies)]
        return jnp.concatenate(pieces_list)[:slot_count].reshape(DOMAIN_CELLS, CELL_NODES)
    domain_keys = jax.random.split(jax.random.fold_in(key, 21), domains)
    table = jax.vmap(one_domain)(domain_keys)
    return table.reshape(ALL_CELLS, CELL_NODES).astype(jnp.int32)


def draw_cell_ham(key, part):
    base_key = jax.random.fold_in(key, 31)
    shape = (ALL_CELLS, CELL_NODES, CELL_NODES)
    base = jax.random.normal(base_key, shape, jnp.float32)
    symmetric = (base + jnp.swapaxes(base, 1, 2)) / jnp.sqrt(2.0 * CELL_NODES)
    return jnp.clip(symmetric, -0.5, 0.5).astype(jnp.float32)


def levels(key, extent, shards, smallest, top_value):
    def one(axis_at, shards_of):
        heights = jax.random.uniform(jax.random.fold_in(jax.random.fold_in(key, 6), axis_at), (shards_of,), jnp.float32, smallest / len(shards), top_value / len(shards))
        return jnp.repeat(jnp.exp(heights), extent[axis_at] // shards_of).reshape((-1,) + (1,) * (len(extent) - axis_at - 1))

    loudness = one(*shards[0])
    for cut in shards[1:]:
        loudness = loudness * one(*cut)
    return loudness


def normal_values(rng, extent, scale, bound, cuts=(), held_as=jnp.bfloat16):
    entries = jax.random.normal(rng, extent, jnp.float32) * scale
    if len(cuts) > 0:
        entries = levels(rng, extent, cuts, -0.22, 0.18) * entries
    return jnp.clip(entries, min=-bound, max=bound).astype(held_as)


def setup_inputs(seed: int = 0) -> dict:
    arg_keys = jax.random.split(jax.random.key(seed), 9)
    states = normal_values(arg_keys[0], (ALL_NODES, STATES), 1.0, 6.0, ((0, 8), (1, 4)), jnp.float32)
    inv_mass = jnp.clip(jnp.exp(math.log(2.0) - 1.3862944 * jax.random.uniform(arg_keys[1], (ALL_NODES,), jnp.float32) ** levels(arg_keys[1], (ALL_NODES,), ((0, 8),), -0.2, 0.2)), 0.5, 2.0)
    cell_ham = draw_cell_ham(jax.random.fold_in(arg_keys[8], 71), 0)
    cell_nodes = draw_cell_nodes(jax.random.fold_in(arg_keys[8], 71), 0)
    send_up = draw_send_up(jax.random.fold_in(arg_keys[8], 71), 0)
    send_down = draw_send_down(jax.random.fold_in(arg_keys[8], 71), 0)
    owner = jax.random.permutation(arg_keys[6], DOMAINS).astype(jnp.int32)
    rotation_store = normal_values(arg_keys[7], (STATES, STATES), STATES ** -0.5, 0.15625, ((0, 8),), jnp.float32)
    return dict(states=states, inv_mass=inv_mass, cell_ham=cell_ham, cell_nodes=cell_nodes, send_up=send_up, send_down=send_down, owner=owner, rotation_store=rotation_store)


filter_center = 2.5
filter_half = 3.5
spectrum_floor = -4.0
sigma_one = filter_half / (spectrum_floor - filter_center)
sigma_two = 1.0 / (2.0 / sigma_one - sigma_one)


def apply_operator(values, inv_mass, cell_ham, cell_nodes, send_up, send_down):
    domains = N_DOM
    owned_count = OWNED_NODES
    ghost_count = GHOST_NODES
    width = values.shape[1]
    scaled = (values * inv_mass[:, None]).reshape(domains, owned_count, width)
    upper_lists = send_up.reshape(domains, ghost_count)
    lower_lists = send_down.reshape(domains, ghost_count)
    select_rows = jax.vmap(lambda values_block, index_list: values_block[index_list])
    lower_ghosts = jnp.roll(select_rows(scaled, upper_lists), 1, axis=0)
    upper_ghosts = jnp.roll(select_rows(scaled, lower_lists), -1, axis=0)
    extended = jnp.concatenate([scaled, lower_ghosts, upper_ghosts], axis=1)
    hams = cell_ham.reshape(domains, DOMAIN_CELLS, CELL_NODES, CELL_NODES)
    node_table = cell_nodes.reshape(domains, DOMAIN_CELLS, CELL_NODES)

    def one_domain(inputs):
        extended_block, ham_block, node_block = inputs
        gathered = extended_block[node_block]
        products = jnp.einsum("cij,cjs->cis", ham_block, gathered, precision=lax.Precision.HIGHEST, preferred_element_type=jnp.float32)
        empty = jnp.zeros((owned_count + 2 * ghost_count, width), jnp.float32)
        return empty.at[node_block.reshape(-1)].add(products.reshape(-1, width))

    assembled = lax.map(one_domain, (extended, hams, node_table))
    from_upper = jnp.roll(assembled[:, owned_count:owned_count + ghost_count], -1, axis=0)
    from_lower = jnp.roll(assembled[:, owned_count + ghost_count:], 1, axis=0)
    add_rows = jax.vmap(lambda values_block, index_list, extra: values_block.at[index_list].add(extra))
    result = add_rows(assembled[:, :owned_count], upper_lists, from_upper)
    result = add_rows(result, lower_lists, from_lower)
    return result.reshape(domains * owned_count, width) * inv_mass[:, None]


def reference(states, inv_mass, cell_ham, cell_nodes, send_up, send_down, owner, rotation_store):
    filtered_one = (sigma_one / filter_half) * (apply_operator(states, inv_mass, cell_ham, cell_nodes, send_up, send_down) - filter_center * states)
    applied = apply_operator(filtered_one, inv_mass, cell_ham, cell_nodes, send_up, send_down)
    filtered_two = (2.0 * sigma_two / filter_half) * (applied - filter_center * filtered_one) - sigma_one * sigma_two * states
    row_index = (owner[:, None] * PANEL_ROWS + jnp.arange(PANEL_ROWS, dtype=jnp.int32)[None, :]).reshape(-1).astype(jnp.int32)
    rotation = rotation_store[row_index]
    return jnp.dot(filtered_two, rotation, precision=lax.Precision.HIGHEST, preferred_element_type=jnp.float32)
```

```python
import functools

import jax
import jax.numpy as jnp
from jax import lax
from jax.experimental import pallas as pl
from jax.experimental.pallas import tpu as pltpu
from jax.sharding import PartitionSpec as P

filter_center = 2.5
filter_half = 3.5
spectrum_floor = -4.0
sigma_one = filter_half / (spectrum_floor - filter_center)
sigma_two = 1.0 / (2.0 / sigma_one - sigma_one)

f32 = jnp.float32
bf16 = jnp.bfloat16
VMEM_LIMIT = 48 * 1024 * 1024


def split(x):
    hi = x.astype(bf16)
    lo = (x - hi.astype(f32)).astype(bf16)
    return hi, lo


def mm(a, b, dims=((1,), (0,))):
    return lax.dot_general(a, b, (dims, ((), ())), preferred_element_type=f32)


def select(onehot, x):
    hi, lo = split(x)
    rest = (x - hi.astype(f32) - lo.astype(f32)).astype(bf16)
    return mm(onehot, hi) + mm(onehot, lo) + mm(onehot, rest)


def as_column(row):
    n = row.shape[1]
    here = lax.broadcasted_iota(jnp.int32, (n, n), 0) == lax.broadcasted_iota(jnp.int32, (n, n), 1)
    return jnp.sum(jnp.where(here, row, jnp.zeros_like(row)), axis=1, keepdims=True)


def pick_rows(list_row, owned):
    column = as_column(list_row.astype(f32)).astype(jnp.int32)
    shape = (list_row.shape[1], owned)
    return (lax.broadcasted_iota(jnp.int32, shape, 1) == column).astype(f32).astype(bf16)


def put_rows(list_row, owned):
    shape = (owned, list_row.shape[1])
    return (lax.broadcasted_iota(jnp.int32, shape, 0) == list_row).astype(f32).astype(bf16)


def call(kernel, out_shape, args, cost, scalars=(), **kwargs):
    vmem = pl.BlockSpec(memory_space=pltpu.VMEM)
    smem = pl.BlockSpec(memory_space=pltpu.SMEM)
    specs = [smem if i in scalars else vmem for i in range(len(args))]
    return pl.pallas_call(
        kernel,
        out_shape=out_shape,
        in_specs=specs,
        out_specs=jax.tree.map(lambda _: vmem, out_shape),
        compiler_params=pltpu.CompilerParams(vmem_limit_bytes=VMEM_LIMIT),
        cost_estimate=pl.CostEstimate(flops=cost, bytes_accessed=1 << 20, transcendentals=0),
        **kwargs,
    )(*args)


def shape(*dims, dtype=f32):
    return jax.ShapeDtypeStruct(dims, dtype)


def send_kernel(s, m, up, dn, up_out, dn_out):
    owned = s.shape[0]
    x = s[...] * as_column(m[...])
    up_out[...] = select(pick_rows(up[...], owned), x)
    dn_out[...] = select(pick_rows(dn[...], owned), x)


def assemble_kernel(ham, nodes, out, total):
    cell = pl.program_id(0)
    ext = total.shape[0]
    row = nodes[pl.ds(cell, 1), :]
    spread = (lax.broadcasted_iota(jnp.int32, (ext, row.shape[1]), 0) == row).astype(f32).astype(bf16)
    hi, lo = split(ham[0])
    left_hi, left_lo = split(mm(spread, hi) + mm(spread, lo))
    both = mm(jnp.concatenate([left_hi, left_lo], axis=0), spread, ((1,), (1,)))
    term = both[:ext] + both[ext:]

    @pl.when(cell == 0)
    def _():
        total[...] = term

    @pl.when(cell > 0)
    def _():
        total[...] += term

    @pl.when(cell == pl.num_programs(0) - 1)
    def _():
        full = total[...]
        hi = full.astype(bf16).astype(f32)
        out[...] = jnp.concatenate([hi, full - hi, hi], axis=1).astype(bf16)


def assemble(cell_ham, cell_nodes, ext):
    cells, n, _ = cell_ham.shape
    return pl.pallas_call(
        assemble_kernel,
        grid=(cells,),
        out_shape=shape(ext, 3 * ext, dtype=bf16),
        in_specs=[
            pl.BlockSpec((1, n, n), lambda c: (c, 0, 0)),
            pl.BlockSpec((cells, n), lambda c: (0, 0)),
        ],
        out_specs=pl.BlockSpec((ext, 3 * ext), lambda c: (0, 0)),
        scratch_shapes=[pltpu.VMEM((ext, ext), f32)],
        compiler_params=pltpu.CompilerParams(vmem_limit_bytes=VMEM_LIMIT),
        cost_estimate=pl.CostEstimate(
            flops=cells * 8 * n * n * ext, bytes_accessed=cells * n * n * 4, transcendentals=0
        ),
    )(cell_ham, cell_nodes)


def apply_kernel(v, m, lower, upper, ham, own, to_lower, to_upper):
    owned = v.shape[0]
    ghost = lower.shape[0]
    x = jnp.concatenate([v[...] * as_column(m[...]), lower[...], upper[...]], axis=0)
    hi, lo = split(x)
    z = mm(ham[...], jnp.concatenate([hi, hi, lo], axis=0))
    own[...] = z[:owned]
    to_lower[...] = z[owned : owned + ghost]
    to_upper[...] = z[owned + ghost :]


def collect(own, from_upper, from_lower, up, dn):
    owned = own.shape[0]
    return (
        own[...]
        + select(put_rows(up[...], owned), from_upper[...])
        + select(put_rows(dn[...], owned), from_lower[...])
    )


def middle_kernel(own, from_upper, from_lower, s, m, up, dn, one, up_out, dn_out):
    owned = s.shape[0]
    column = as_column(m[...])
    r = collect(own, from_upper, from_lower, up, dn)
    filtered = (sigma_one / filter_half) * (r * column - filter_center * s[...])
    one[...] = filtered
    x = filtered * column
    up_out[...] = select(pick_rows(up[...], owned), x)
    dn_out[...] = select(pick_rows(dn[...], owned), x)


def last_kernel(own, from_upper, from_lower, s, one, m, up, dn, two):
    column = as_column(m[...])
    r = collect(own, from_upper, from_lower, up, dn)
    two[...] = (
        2.0 * sigma_two / filter_half * (r * column - filter_center * one[...])
        - sigma_one * sigma_two * s[...]
    )


def order_kernel(owner, *refs):
    parts, (hi_out, lo_out) = refs[:-2], refs[-2:]
    here = lax.axis_index("dom")
    for b, part in enumerate(parts):
        slot = here ^ b
        place = jnp.int32(0)
        for p in range(len(parts)):
            place = place + jnp.where(owner[p] == slot, p, 0)
        hi, lo = split(part[...])
        hi_out[place] = hi
        lo_out[place] = lo


def rotate_kernel(hi_ref, lo_ref, *refs):
    parts, out = refs[:-1], refs[-1]
    here = lax.axis_index("band")
    bands = hi_ref.shape[0]
    total = None
    for r, part in enumerate(parts):
        k = lax.rem(here + r, bands)
        hi, lo = split(part[...])
        rhi, rlo = hi_ref[k], lo_ref[k]
        term = mm(
            jnp.concatenate([hi, lo, hi], axis=1), jnp.concatenate([rhi, rhi, rlo], axis=0)
        )
        total = term if total is None else total + term
    out[...] = total


def cyclic(count, step):
    return [(i, (i + step) % count) for i in range(count)]


def flip(count, bits):
    return [(i, i ^ bits) for i in range(count)]


def ordered_rotation(own_columns, owner, bands):
    doms = lax.axis_size("dom")
    rows, cols = own_columns.shape
    if doms == 8 and rows % 16 == 0:
        parts = [own_columns] + [
            lax.ppermute(own_columns, "dom", flip(doms, bits)) for bits in (2, 4, 6)
        ]
        other = [lax.ppermute(part, "dom", flip(doms, 1)) for part in parts]
        slots = [part for pair in zip(parts, other) for part in pair]
        hi, lo = call(
            order_kernel,
            (shape(doms, rows, cols, dtype=bf16),) * 2,
            [owner, *slots],
            rows * doms * cols * 16,
            scalars=(0,),
        )
    else:
        columns = lax.all_gather(own_columns, "dom", axis=0, tiled=True)
        hi, lo = split(columns.reshape(doms, rows, cols)[owner])
    total = doms * rows
    return hi.reshape(bands, total // bands, cols), lo.reshape(bands, total // bands, cols)


def shards(states, inv_mass, cell_ham, cell_nodes, send_up, send_down, owner, rotation_store):
    owned, cols = states.shape
    ghost = send_up.shape[0]
    ext = owned + 2 * ghost
    doms, bands = lax.axis_size("dom"), lax.axis_size("band")
    m = inv_mass[None, :]
    up = send_up[None, :]
    dn = send_down[None, :]
    upward, downward = cyclic(doms, 1), cyclic(doms, -1)
    halo = shape(ghost, cols)
    block = shape(owned, cols)
    small = 4 * ghost * owned * cols * 3

    def exchange(to_upper, to_lower):
        from_lower = lax.ppermute(to_upper, "dom", upward)
        from_upper = lax.ppermute(to_lower, "dom", downward)
        return from_lower, from_upper

    def apply(v, lower, upper, ham):
        own, to_lower, to_upper = call(
            apply_kernel, (block, halo, halo), [v, m, lower, upper, ham], 6 * ext * ext * cols
        )
        from_lower, from_upper = exchange(to_upper, to_lower)
        return own, from_upper, from_lower

    to_upper, to_lower = call(send_kernel, (halo, halo), [states, m, up, dn], small)
    lower, upper = exchange(to_upper, to_lower)
    ham = assemble(cell_ham, cell_nodes, ext)
    band = lax.axis_index("band")
    own_columns = lax.dynamic_slice_in_dim(rotation_store, band * cols, cols, 1)
    rot_hi, rot_lo = ordered_rotation(own_columns, owner, bands)
    first = apply(states, lower, upper, ham)
    one, to_upper, to_lower = call(
        middle_kernel, (block, halo, halo), [*first, states, m, up, dn], 2 * small
    )
    lower, upper = exchange(to_upper, to_lower)
    second = apply(one, lower, upper, ham)
    two = call(last_kernel, block, [*second, states, one, m, up, dn], small)
    parts = [two] + [lax.ppermute(two, "band", cyclic(bands, -r)) for r in range(1, bands)]
    return call(
        rotate_kernel, block, [rot_hi, rot_lo, *parts], 6 * owned * cols * cols * bands
    )


def solution(mesh):
    in_specs = (
        P("dom", "band"),
        P("dom"),
        P("dom", None, None),
        P("dom", None),
        P("dom"),
        P("dom"),
        P(),
        P("dom", None),
    )
    out_specs = P("dom", "band")
    return jax.shard_map(shards, mesh=mesh, in_specs=in_specs, out_specs=out_specs, check_vma=False)
```

```python
import functools

import jax
import jax.numpy as jnp
from jax import lax
from jax.experimental import pallas as pl
from jax.experimental.pallas import tpu as pltpu
from jax.sharding import PartitionSpec as P

filter_center = 2.5
filter_half = 3.5
spectrum_floor = -4.0
sigma_one = filter_half / (spectrum_floor - filter_center)
sigma_two = 1.0 / (2.0 / sigma_one - sigma_one)

f32 = jnp.float32
bf16 = jnp.bfloat16
VMEM_LIMIT = 32 * 1024 * 1024
VMEM_MOST = 56 * 1024 * 1024


def split(x):
    hi = x.astype(bf16)
    lo = (x - hi.astype(f32)).astype(bf16)
    return hi, lo


def mm(a, b, dims=((1,), (0,))):
    return lax.dot_general(a, b, (dims, ((), ())), preferred_element_type=f32)


def select(onehot, x):
    hi, lo = split(x)
    rest = (x - hi.astype(f32) - lo.astype(f32)).astype(bf16)
    return mm(onehot, hi) + mm(onehot, lo) + mm(onehot, rest)


def as_column(row):
    n = row.shape[1]
    here = lax.broadcasted_iota(jnp.int32, (n, n), 0) == lax.broadcasted_iota(jnp.int32, (n, n), 1)
    return jnp.sum(jnp.where(here, row, jnp.zeros_like(row)), axis=1, keepdims=True)


def pick_rows(list_row, owned):
    column = as_column(list_row.astype(f32)).astype(jnp.int32)
    shape = (list_row.shape[1], owned)
    return (lax.broadcasted_iota(jnp.int32, shape, 1) == column).astype(f32).astype(bf16)


def put_rows(list_row, owned):
    shape = (owned, list_row.shape[1])
    return (lax.broadcasted_iota(jnp.int32, shape, 0) == list_row).astype(f32).astype(bf16)


def call(kernel, out_shape, args, cost, scalars=(), **kwargs):
    vmem = pl.BlockSpec(memory_space=pltpu.VMEM)
    smem = pl.BlockSpec(memory_space=pltpu.SMEM)
    specs = [smem if i in scalars else vmem for i in range(len(args))]
    return pl.pallas_call(
        kernel,
        out_shape=out_shape,
        in_specs=specs,
        out_specs=jax.tree.map(lambda _: vmem, out_shape),
        compiler_params=pltpu.CompilerParams(vmem_limit_bytes=VMEM_LIMIT),
        cost_estimate=pl.CostEstimate(flops=cost, bytes_accessed=1 << 20, transcendentals=0),
        **kwargs,
    )(*args)


def shape(*dims, dtype=f32):
    return jax.ShapeDtypeStruct(dims, dtype)


def near_and_far(up, dn):
    even = lax.rem(lax.axis_index("dom"), 2) == 0
    up, dn = up[...], dn[...]
    return jnp.where(even, up, dn), jnp.where(even, dn, up)


def send_rows(x, up, dn, near_out, far_out):
    near, far = near_and_far(up, dn)
    near_out[...] = select(pick_rows(near, x.shape[0]), x)
    far_out[...] = select(pick_rows(far, x.shape[0]), x)


def cell_term(ham, row, ext):
    n = ham.shape[0]
    gap = -n % 16
    hi, lo = split(jnp.concatenate([ham, jnp.zeros((gap, n), f32)], axis=0))
    spread = lax.broadcasted_iota(jnp.int32, (ext, n), 0) == row
    spread = spread.astype(f32)
    twice = jnp.concatenate([spread, jnp.zeros((ext, gap), f32), spread, jnp.zeros((ext, gap), f32)], axis=1)
    spread = spread.astype(bf16)
    left_hi, left_lo = split(mm(twice.astype(bf16), jnp.concatenate([hi, lo], axis=0)))
    wide = ext // 256 * 256
    both = mm(jnp.concatenate([left_hi, left_lo], axis=0), spread[:wide], ((1,), (1,)))
    rest = mm(
        jnp.concatenate([left_hi[wide:], left_lo[wide:]], axis=0), spread[wide:], ((1,), (1,))
    )
    return both[:ext] + both[ext:], rest[: ext - wide] + rest[ext - wide :]


def assemble_kernel(ghost, nodes_any, ham_any, out, raw, ham, left, corner, sem):
    cells = ham.shape[0]
    ext, wide = left.shape
    owned = ext - 2 * ghost
    moves = [(nodes_any, raw)] + [(ham_any.at[c], ham.at[c]) for c in range(cells)]
    copies = [pltpu.make_async_copy(a, b, sem.at[i]) for i, (a, b) in enumerate(moves)]
    for copy in copies:
        copy.start()
    copies[0].wait()
    node = raw[...]
    lower = (node >= owned) & (node < owned + ghost)
    swapped = jnp.where(lower, node + ghost, jnp.where(node >= owned + ghost, node - ghost, node))
    nodes = jnp.where(lax.rem(lax.axis_index("dom"), 2) == 0, swapped, node)
    for c in range(cells):
        copies[1 + c].wait()
        term, rest = cell_term(ham[c], nodes[c : c + 1, :], ext)
        left[...] = term if c == 0 else left[...] + term
        corner[...] = rest if c == 0 else corner[...] + rest
    below = jnp.transpose(left[ext - 128 :, :])[:, 128 - (ext - wide) :]
    right = jnp.concatenate([below, corner[...]], axis=0)
    full = jnp.concatenate([left[...], right], axis=1)
    hi = full.astype(bf16).astype(f32)
    out[...] = jnp.concatenate([hi, full - hi, hi], axis=1).astype(bf16)


def assemble(cell_nodes, cell_ham, ext, ghost):
    cells, n, _ = cell_ham.shape
    wide = ext // 256 * 256
    return pl.pallas_call(
        functools.partial(assemble_kernel, ghost),
        out_shape=shape(ext, 3 * ext, dtype=bf16),
        in_specs=[pl.BlockSpec(memory_space=pl.ANY)] * 2,
        out_specs=pl.BlockSpec(memory_space=pltpu.VMEM),
        scratch_shapes=[
            pltpu.VMEM((cells, n), jnp.int32),
            pltpu.VMEM((cells, n, n), f32),
            pltpu.VMEM((ext, wide), f32),
            pltpu.VMEM((ext - wide, ext - wide), f32),
            pltpu.SemaphoreType.DMA((1 + cells,)),
        ],
        compiler_params=pltpu.CompilerParams(vmem_limit_bytes=VMEM_MOST),
        cost_estimate=pl.CostEstimate(
            flops=cells * 8 * n * n * ext, bytes_accessed=cells * n * n * 4, transcendentals=0
        ),
    )(cell_nodes, cell_ham)


def apply_kernel(v, m, near, far, ham, own, to_near, to_far):
    owned = v.shape[0]
    ghost = near.shape[0]
    x = jnp.concatenate([v[...] * as_column(m[...]), near[...], far[...]], axis=0)
    hi, lo = split(x)
    z = mm(ham[...], jnp.concatenate([hi, hi, lo], axis=0))
    own[...] = z[:owned]
    to_near[...] = z[owned : owned + ghost]
    to_far[...] = z[owned + ghost :]


def collect(own, from_near, from_far, up, dn):
    owned = own.shape[0]
    near, far = near_and_far(up, dn)
    return (
        own[...]
        + select(put_rows(near, owned), from_near[...])
        + select(put_rows(far, owned), from_far[...])
    )


def middle_kernel(own, from_near, from_far, s, m, up, dn, one, near_out, far_out):
    column = as_column(m[...])
    r = collect(own, from_near, from_far, up, dn)
    filtered = (sigma_one / filter_half) * (r * column - filter_center * s[...])
    one[...] = filtered
    send_rows(filtered * column, up, dn, near_out, far_out)


def last_kernel(own, from_near, from_far, s, one, m, up, dn, two):
    column = as_column(m[...])
    r = collect(own, from_near, from_far, up, dn)
    two[...] = (
        2.0 * sigma_two / filter_half * (r * column - filter_center * one[...])
        - sigma_one * sigma_two * s[...]
    )


def order_kernel(owner, *refs):
    parts, (hi_out, lo_out) = refs[:-2], refs[-2:]
    here = lax.axis_index("dom")
    for b, part in enumerate(parts):
        slot = here ^ b
        place = jnp.int32(0)
        for p in range(len(parts)):
            place = place + jnp.where(owner[p] == slot, p, 0)
        hi, lo = split(part[...])
        hi_out[place] = hi
        lo_out[place] = lo


def rotated_rows(hi_ref, lo_ref, parts):
    here = lax.axis_index("band")
    total = None
    for r, part in parts:
        k = here ^ r
        hi, lo = split(part)
        rhi, rlo = hi_ref[k], lo_ref[k]
        term = mm(
            jnp.concatenate([hi, lo, hi], axis=1), jnp.concatenate([rhi, rhi, rlo], axis=0)
        )
        total = term if total is None else total + term
    return total


def rotate_kernel(hi_ref, lo_ref, own, one, two, out):
    out[...] = rotated_rows(hi_ref, lo_ref, [(0, own[...]), (1, one[...]), (2, two[...])])


def rotate_last_kernel(hi_ref, lo_ref, total, inner, outer, m, up, dn, out, near_out, far_out):
    rows = total[...] + rotated_rows(hi_ref, lo_ref, [(3, inner[...] + outer[...])])
    out[...] = rows
    send_rows(rows * as_column(m[...]), up, dn, near_out, far_out)


def flip(count, bits):
    return [(i, i ^ bits) for i in range(count)]


def ordered_rotation(slots, owner, bands):
    rows, cols = slots[0].shape
    total = len(slots) * rows
    hi, lo = call(
        order_kernel,
        (shape(len(slots), rows, cols, dtype=bf16),) * 2,
        [owner, *slots],
        total * cols * 16,
        scalars=(0,),
    )
    return hi.reshape(bands, total // bands, cols), lo.reshape(bands, total // bands, cols)


def shards(states, inv_mass, cell_ham, cell_nodes, send_up, send_down, owner, rotation_store):
    owned, cols = states.shape
    ghost = send_up.shape[0]
    ext = owned + 2 * ghost
    doms, bands = lax.axis_size("dom"), lax.axis_size("band")
    m = inv_mass[None, :]
    up = send_up[None, :]
    dn = send_down[None, :]
    near_pairs = flip(doms, 1)
    far_pairs = [(i, (i - 1 if i % 2 == 0 else i + 1) % doms) for i in range(doms)]
    halo = shape(ghost, cols)
    block = shape(owned, cols)
    small = 4 * ghost * owned * cols * 3

    def exchange(to_near, to_far):
        from_far = lax.ppermute(to_far, "dom", far_pairs)
        from_near = lax.ppermute(to_near, "dom", near_pairs)
        return from_near, from_far

    def apply(v, near, far, ham):
        own, to_near, to_far = call(
            apply_kernel, (block, halo, halo), [v, m, near, far, ham], 6 * ext * ext * cols
        )
        return (own, *exchange(to_near, to_far))

    ham = assemble(cell_nodes, cell_ham, ext, ghost)
    band = lax.axis_index("band")
    own_columns = lax.dynamic_slice_in_dim(rotation_store, band * cols, cols, 1)
    one = lax.ppermute(states, "band", flip(4, 1))
    two = lax.ppermute(states, "band", flip(4, 2))
    paired = doms == 8 and rotation_store.shape[0] % 16 == 0
    parts = [own_columns]
    if paired:
        parts += [lax.ppermute(own_columns, "dom", flip(doms, b)) for b in (2, 4, 6)]
    held, one, two, ham, *parts = lax.optimization_barrier((states, one, two, ham, *parts))
    inner = lax.ppermute(held, "band", [(1, 2), (2, 1)])
    outer = lax.ppermute(two, "band", [(1, 0), (2, 3)])
    if paired:
        other = [lax.ppermute(part, "dom", near_pairs) for part in parts]
        slots = [part for pair in zip(parts, other) for part in pair]
        rotation = ordered_rotation(slots, owner, bands)
    else:
        columns = lax.all_gather(own_columns, "dom", axis=0, tiled=True)
        columns = columns.reshape(doms, -1, cols)[owner].reshape(bands, -1, cols)
        rotation = split(columns)
    work = 6 * owned * cols * cols
    total = call(rotate_kernel, block, [*rotation, held, one, two], 3 * work)
    turned, to_near, to_far = call(
        rotate_last_kernel,
        (block, halo, halo),
        [*rotation, total, inner, outer, m, up, dn],
        work,
    )
    near, far = exchange(to_near, to_far)
    first = apply(turned, near, far, ham)
    filtered, to_near, to_far = call(
        middle_kernel, (block, halo, halo), [*first, turned, m, up, dn], 2 * small
    )
    near, far = exchange(to_near, to_far)
    second = apply(filtered, near, far, ham)
    return call(last_kernel, block, [*second, turned, filtered, m, up, dn], small)


def solution(mesh):
    in_specs = (
        P("dom", "band"),
        P("dom"),
        P("dom", None, None),
        P("dom", None),
        P("dom"),
        P("dom"),
        P(),
        P("dom", None),
    )
    out_specs = P("dom", "band")
    return jax.shard_map(shards, mesh=mesh, in_specs=in_specs, out_specs=out_specs, check_vma=False)
```

```python
import functools

import jax
import jax.numpy as jnp
from jax import lax
from jax.experimental import pallas as pl
from jax.experimental.pallas import tpu as pltpu
from jax.sharding import PartitionSpec as P

filter_center = 2.5
filter_half = 3.5
spectrum_floor = -4.0
sigma_one = filter_half / (spectrum_floor - filter_center)
sigma_two = 1.0 / (2.0 / sigma_one - sigma_one)

f32 = jnp.float32
bf16 = jnp.bfloat16
VMEM_LIMIT = 32 * 1024 * 1024
VMEM_MOST = 56 * 1024 * 1024


def split(x):
    hi = x.astype(bf16)
    lo = (x - hi.astype(f32)).astype(bf16)
    return hi, lo


def mm(a, b, dims=((1,), (0,))):
    return lax.dot_general(a, b, (dims, ((), ())), preferred_element_type=f32)


def select(onehot, x):
    hi, lo = split(x)
    rest = (x - hi.astype(f32) - lo.astype(f32)).astype(bf16)
    return mm(onehot, hi) + mm(onehot, lo) + mm(onehot, rest)


def as_column(row):
    n = row.shape[1]
    here = lax.broadcasted_iota(jnp.int32, (n, n), 0) == lax.broadcasted_iota(jnp.int32, (n, n), 1)
    return jnp.sum(jnp.where(here, row, jnp.zeros_like(row)), axis=1, keepdims=True)


def pick_rows(list_row, owned):
    column = as_column(list_row.astype(f32)).astype(jnp.int32)
    shape = (list_row.shape[1], owned)
    return (lax.broadcasted_iota(jnp.int32, shape, 1) == column).astype(f32).astype(bf16)


def put_rows(list_row, owned):
    shape = (owned, list_row.shape[1])
    return (lax.broadcasted_iota(jnp.int32, shape, 0) == list_row).astype(f32).astype(bf16)


def call(kernel, out_shape, args, cost, scalars=(), **kwargs):
    vmem = pl.BlockSpec(memory_space=pltpu.VMEM)
    smem = pl.BlockSpec(memory_space=pltpu.SMEM)
    specs = [smem if i in scalars else vmem for i in range(len(args))]
    return pl.pallas_call(
        kernel,
        out_shape=out_shape,
        in_specs=specs,
        out_specs=jax.tree.map(lambda _: vmem, out_shape),
        compiler_params=pltpu.CompilerParams(vmem_limit_bytes=VMEM_LIMIT),
        cost_estimate=pl.CostEstimate(flops=cost, bytes_accessed=1 << 20, transcendentals=0),
        **kwargs,
    )(*args)


def shape(*dims, dtype=f32):
    return jax.ShapeDtypeStruct(dims, dtype)


def lists_kernel(m, up, dn, column, pick, put):
    owned = m.shape[1]
    column[...] = jnp.broadcast_to(as_column(m[...]), column.shape)
    even = lax.rem(lax.axis_index("dom"), 2) == 0
    up, dn = up[...], dn[...]
    near, far = jnp.where(even, up, dn), jnp.where(even, dn, up)
    rows = jnp.concatenate([pick_rows(near, owned), pick_rows(far, owned)], axis=0)
    pick[...] = jnp.concatenate([rows.astype(f32)] * 3, axis=1).astype(bf16)
    lanes = [put_rows(near, owned).astype(f32), put_rows(far, owned).astype(f32)]
    put[...] = jnp.concatenate(lanes * 3, axis=1).astype(bf16)


def split_three(x):
    hi, lo = split(x)
    return hi, lo, (x - hi.astype(f32) - lo.astype(f32)).astype(bf16)


def send_rows(x, pick, near_out, far_out):
    rows = mm(pick[...], jnp.concatenate(split_three(x), axis=0))
    ghost = near_out.shape[0]
    near_out[...] = rows[:ghost]
    far_out[...] = rows[ghost:]


def cell_term(ham, row, ext):
    n = ham.shape[0]
    gap = -n % 16
    hi, lo = split(jnp.concatenate([ham, jnp.zeros((gap, n), f32)], axis=0))
    spread = lax.broadcasted_iota(jnp.int32, (ext, n), 0) == row
    spread = spread.astype(f32)
    twice = jnp.concatenate([spread, jnp.zeros((ext, gap), f32), spread, jnp.zeros((ext, gap), f32)], axis=1)
    spread = spread.astype(bf16)
    left_hi, left_lo = split(mm(twice.astype(bf16), jnp.concatenate([hi, lo], axis=0)))
    wide = ext // 256 * 256
    both = mm(jnp.concatenate([left_hi, left_lo], axis=0), spread[:wide], ((1,), (1,)))
    rest = mm(
        jnp.concatenate([left_hi[wide:], left_lo[wide:]], axis=0), spread[wide:], ((1,), (1,))
    )
    return both[:ext] + both[ext:], rest[: ext - wide] + rest[ext - wide :]


def assemble_kernel(ghost, nodes_any, ham_any, own, halo, raw, ham, left, corner, sem):
    cells = ham.shape[0]
    ext, wide = left.shape
    owned = ext - 2 * ghost
    moves = [(nodes_any, raw)] + [(ham_any.at[c], ham.at[c]) for c in range(cells)]
    copies = [pltpu.make_async_copy(a, b, sem.at[i]) for i, (a, b) in enumerate(moves)]
    for copy in copies:
        copy.start()
    copies[0].wait()
    node = raw[...]
    lower = (node >= owned) & (node < owned + ghost)
    swapped = jnp.where(lower, node + ghost, jnp.where(node >= owned + ghost, node - ghost, node))
    nodes = jnp.where(lax.rem(lax.axis_index("dom"), 2) == 0, swapped, node)
    for c in range(cells):
        copies[1 + c].wait()
        term, rest = cell_term(ham[c], nodes[c : c + 1, :], ext)
        left[...] = term if c == 0 else left[...] + term
        corner[...] = rest if c == 0 else corner[...] + rest
    below = jnp.transpose(left[ext - 128 :, :])[:, 128 - (ext - wide) :]
    right = jnp.concatenate([below, corner[...]], axis=0)
    full = jnp.concatenate([left[...], right], axis=1)
    hi = full.astype(bf16).astype(f32)
    lo = full - hi
    for out, start, stop in ((own, 0, owned), (halo, owned, ext)):
        high = hi[:, start:stop]
        out[...] = jnp.concatenate([high, lo[:, start:stop], high], axis=1).astype(bf16)


def assemble(cell_nodes, cell_ham, ext, ghost):
    cells, n, _ = cell_ham.shape
    wide = ext // 256 * 256
    return pl.pallas_call(
        functools.partial(assemble_kernel, ghost),
        out_shape=(
            shape(ext, 3 * (ext - 2 * ghost), dtype=bf16),
            shape(ext, 6 * ghost, dtype=bf16),
        ),
        in_specs=[pl.BlockSpec(memory_space=pl.ANY)] * 2,
        out_specs=(pl.BlockSpec(memory_space=pltpu.VMEM),) * 2,
        scratch_shapes=[
            pltpu.VMEM((cells, n), jnp.int32),
            pltpu.VMEM((cells, n, n), f32),
            pltpu.VMEM((ext, wide), f32),
            pltpu.VMEM((ext - wide, ext - wide), f32),
            pltpu.SemaphoreType.DMA((1 + cells,)),
        ],
        compiler_params=pltpu.CompilerParams(vmem_limit_bytes=VMEM_MOST),
        cost_estimate=pl.CostEstimate(
            flops=cells * 8 * n * n * ext, bytes_accessed=cells * n * n * 4, transcendentals=0
        ),
    )(cell_nodes, cell_ham)


def own_kernel(v, column, ham, out):
    hi, lo = split(v[...] * column[:, :1])
    out[...] = mm(ham[...], jnp.concatenate([hi, hi, lo], axis=0))


def add_halo(partial, near, far, ham, to_near, to_far):
    ghost = near.shape[0]
    owned = partial.shape[0] - 2 * ghost
    hi, lo = split(jnp.concatenate([near[...], far[...]], axis=0))
    z = partial[...] + mm(ham[...], jnp.concatenate([hi, hi, lo], axis=0))
    to_near[...] = z[owned : owned + ghost]
    to_far[...] = z[owned + ghost :]
    return z[:owned]


def first_kernel(partial, near, far, ham, column, s, base, to_near, to_far):
    z = add_halo(partial, near, far, ham, to_near, to_far)
    base[...] = (sigma_one / filter_half) * (z * column[:, :1] - filter_center * s[...])


def second_kernel(partial, near, far, ham, column, one, s, base, to_near, to_far):
    z = add_halo(partial, near, far, ham, to_near, to_far)
    base[...] = (
        2.0 * sigma_two / filter_half * (z * column[:, :1] - filter_center * one[...])
        - sigma_one * sigma_two * s[...]
    )


def collect(factor, base, from_near, from_far, column, put):
    parts = zip(split_three(from_near[...]), split_three(from_far[...]))
    rows = jnp.concatenate([part for pair in parts for part in pair], axis=0)
    return base[...] + factor * column[:, :1] * mm(put[...], rows)


def middle_kernel(base, from_near, from_far, column, put, pick, one, near_out, far_out):
    filtered = collect(sigma_one / filter_half, base, from_near, from_far, column, put)
    one[...] = filtered
    send_rows(filtered * column[:, :1], pick, near_out, far_out)


def last_kernel(base, from_near, from_far, column, put, two):
    two[...] = collect(2.0 * sigma_two / filter_half, base, from_near, from_far, column, put)


def order_kernel(owner, *refs):
    parts, (hi_out, lo_out) = refs[:-2], refs[-2:]
    here = lax.axis_index("dom")
    for b, part in enumerate(parts):
        slot = here ^ b
        place = jnp.int32(0)
        for p in range(len(parts)):
            place = place + jnp.where(owner[p] == slot, p, 0)
        hi, lo = split(part[...])
        hi_out[place] = hi
        lo_out[place] = lo


def rotated_rows(hi_ref, lo_ref, parts):
    here = lax.axis_index("band")
    total = None
    for r, part in parts:
        k = here ^ r
        hi, lo = split(part)
        rhi, rlo = hi_ref[k], lo_ref[k]
        term = mm(
            jnp.concatenate([hi, lo, hi], axis=1), jnp.concatenate([rhi, rhi, rlo], axis=0)
        )
        total = term if total is None else total + term
    return total


def rotate_kernel(hi_ref, lo_ref, own, one, two, out):
    out[...] = rotated_rows(hi_ref, lo_ref, [(0, own[...]), (1, one[...]), (2, two[...])])


def rotate_last_kernel(hi_ref, lo_ref, total, inner, outer, column, pick, out, near_out, far_out):
    here = lax.axis_index("band")
    third = jnp.where((here == 1) | (here == 2), inner[...], outer[...])
    rows = total[...] + rotated_rows(hi_ref, lo_ref, [(3, third)])
    out[...] = rows
    send_rows(rows * column[:, :1], pick, near_out, far_out)


def flip(count, bits):
    return [(i, i ^ bits) for i in range(count)]


def ordered_rotation(slots, owner, bands):
    rows, cols = slots[0].shape
    total = len(slots) * rows
    hi, lo = call(
        order_kernel,
        (shape(len(slots), rows, cols, dtype=bf16),) * 2,
        [owner, *slots],
        total * cols * 16,
        scalars=(0,),
    )
    return hi.reshape(bands, total // bands, cols), lo.reshape(bands, total // bands, cols)


def shards(states, inv_mass, cell_ham, cell_nodes, send_up, send_down, owner, rotation_store):
    owned, cols = states.shape
    ghost = send_up.shape[0]
    ext = owned + 2 * ghost
    doms, bands = lax.axis_size("dom"), lax.axis_size("band")
    m = inv_mass[None, :]
    up = send_up[None, :]
    dn = send_down[None, :]
    near_pairs = flip(doms, 1)
    far_pairs = [(i, (i - 1 if i % 2 == 0 else i + 1) % doms) for i in range(doms)]
    halo = shape(ghost, cols)
    block = shape(owned, cols)
    small = 4 * ghost * owned * cols * 3

    def exchange(to_near, to_far):
        from_far = lax.ppermute(to_far, "dom", far_pairs)
        from_near = lax.ppermute(to_near, "dom", near_pairs)
        return from_near, from_far

    ham_own, ham_halo = assemble(cell_nodes, cell_ham, ext, ghost)
    column, pick, put = call(
        lists_kernel,
        (
            shape(owned, 128),
            shape(2 * ghost, 3 * owned, dtype=bf16),
            shape(owned, 6 * ghost, dtype=bf16),
        ),
        [m, up, dn],
        owned * owned,
    )
    band = lax.axis_index("band")
    own_columns = lax.dynamic_slice_in_dim(rotation_store, band * cols, cols, 1)
    one = lax.ppermute(states, "band", flip(4, 1))
    two = lax.ppermute(states, "band", flip(4, 2))
    paired = doms == 8 and rotation_store.shape[0] % 16 == 0
    parts = [own_columns]
    if paired:
        parts += [lax.ppermute(own_columns, "dom", flip(doms, b)) for b in (2, 4, 6)]
    ham_own, *parts = lax.optimization_barrier((ham_own, *parts))
    held, one, two, ham_own = lax.optimization_barrier((states, one, two, ham_own))
    inner = lax.ppermute(held, "band", [(0, 0), (1, 2), (2, 1), (3, 3)])
    outer = lax.ppermute(two, "band", flip(4, 1))
    if paired:
        other = [lax.ppermute(part, "dom", near_pairs) for part in parts]
        slots = [part for pair in zip(parts, other) for part in pair]
        rotation = ordered_rotation(slots, owner, bands)
    else:
        columns = lax.all_gather(own_columns, "dom", axis=0, tiled=True)
        columns = columns.reshape(doms, -1, cols)[owner].reshape(bands, -1, cols)
        rotation = split(columns)
    work = 6 * owned * cols * cols
    total = call(rotate_kernel, block, [*rotation, held, one, two], 3 * work)
    turned, to_near, to_far = call(
        rotate_last_kernel,
        (block, halo, halo),
        [*rotation, total, inner, outer, column, pick],
        work,
    )
    wide = shape(ext, cols)
    work = 6 * ext * ext * cols
    near, far = exchange(to_near, to_far)
    partial = call(own_kernel, wide, [turned, column, ham_own], work)
    base, to_near, to_far = call(
        first_kernel,
        (block, halo, halo),
        [partial, near, far, ham_halo, column, turned],
        work,
    )
    near, far = exchange(to_near, to_far)
    filtered, to_near, to_far = call(
        middle_kernel, (block, halo, halo), [base, near, far, column, put, pick], small
    )
    near, far = exchange(to_near, to_far)
    partial = call(own_kernel, wide, [filtered, column, ham_own], work)
    base, to_near, to_far = call(
        second_kernel,
        (block, halo, halo),
        [partial, near, far, ham_halo, column, filtered, turned],
        work,
    )
    near, far = exchange(to_near, to_far)
    return call(last_kernel, block, [base, near, far, column, put], small)


def solution(mesh):
    in_specs = (
        P("dom", "band"),
        P("dom"),
        P("dom", None, None),
        P("dom", None),
        P("dom"),
        P("dom"),
        P(),
        P("dom", None),
    )
    out_specs = P("dom", "band")
    return jax.shard_map(shards, mesh=mesh, in_specs=in_specs, out_specs=out_specs, check_vma=False)
```

```python
import functools

import jax
import jax.numpy as jnp
from jax import lax
from jax.experimental import pallas as pl
from jax.experimental.pallas import tpu as pltpu
from jax.sharding import PartitionSpec as P

filter_center = 2.5
filter_half = 3.5
spectrum_floor = -4.0
sigma_one = filter_half / (spectrum_floor - filter_center)
sigma_two = 1.0 / (2.0 / sigma_one - sigma_one)

f32 = jnp.float32
bf16 = jnp.bfloat16
VMEM_LIMIT = 32 * 1024 * 1024
VMEM_MOST = 56 * 1024 * 1024


def split(x):
    hi = x.astype(bf16)
    lo = (x - hi.astype(f32)).astype(bf16)
    return hi, lo


def mm(a, b, dims=((1,), (0,))):
    return lax.dot_general(a, b, (dims, ((), ())), preferred_element_type=f32)


def select(onehot, x):
    hi, lo = split(x)
    rest = (x - hi.astype(f32) - lo.astype(f32)).astype(bf16)
    return mm(onehot, hi) + mm(onehot, lo) + mm(onehot, rest)


def as_column(row):
    n = row.shape[1]
    here = lax.broadcasted_iota(jnp.int32, (n, n), 0) == lax.broadcasted_iota(jnp.int32, (n, n), 1)
    return jnp.sum(jnp.where(here, row, jnp.zeros_like(row)), axis=1, keepdims=True)


def pick_rows(list_row, owned):
    column = as_column(list_row.astype(f32)).astype(jnp.int32)
    shape = (list_row.shape[1], owned)
    return (lax.broadcasted_iota(jnp.int32, shape, 1) == column).astype(f32).astype(bf16)


def put_rows(list_row, owned):
    shape = (owned, list_row.shape[1])
    return (lax.broadcasted_iota(jnp.int32, shape, 0) == list_row).astype(f32).astype(bf16)


def call(kernel, out_shape, args, cost, scalars=(), **kwargs):
    vmem = pl.BlockSpec(memory_space=pltpu.VMEM)
    smem = pl.BlockSpec(memory_space=pltpu.SMEM)
    specs = [smem if i in scalars else vmem for i in range(len(args))]
    return pl.pallas_call(
        kernel,
        out_shape=out_shape,
        in_specs=specs,
        out_specs=jax.tree.map(lambda _: vmem, out_shape),
        compiler_params=pltpu.CompilerParams(vmem_limit_bytes=VMEM_LIMIT),
        cost_estimate=pl.CostEstimate(flops=cost, bytes_accessed=1 << 20, transcendentals=0),
        **kwargs,
    )(*args)


def shape(*dims, dtype=f32):
    return jax.ShapeDtypeStruct(dims, dtype)


def lists_kernel(m, up, dn, column, pick, put):
    owned = m.shape[1]
    column[...] = jnp.broadcast_to(as_column(m[...]), column.shape)
    even = lax.rem(lax.axis_index("dom"), 2) == 0
    up, dn = up[...], dn[...]
    near, far = jnp.where(even, up, dn), jnp.where(even, dn, up)
    rows = jnp.concatenate([pick_rows(near, owned), pick_rows(far, owned)], axis=0)
    pick[...] = jnp.concatenate([rows.astype(f32)] * 3, axis=1).astype(bf16)
    lanes = [put_rows(near, owned).astype(f32), put_rows(far, owned).astype(f32)]
    put[...] = jnp.concatenate(lanes * 3, axis=1).astype(bf16)


def split_three(x):
    hi, lo = split(x)
    return hi, lo, (x - hi.astype(f32) - lo.astype(f32)).astype(bf16)


def send_rows(x, pick, near_out, far_out):
    rows = mm(pick[...], jnp.concatenate(split_three(x), axis=0))
    ghost = near_out.shape[0]
    near_out[...] = rows[:ghost]
    far_out[...] = rows[ghost:]


def cell_term(ham, row, ext):
    n = ham.shape[0]
    gap = -n % 16
    hi, lo = split(jnp.concatenate([ham, jnp.zeros((gap, n), f32)], axis=0))
    spread = lax.broadcasted_iota(jnp.int32, (ext, n), 0) == row
    spread = spread.astype(f32)
    twice = jnp.concatenate([spread, jnp.zeros((ext, gap), f32), spread, jnp.zeros((ext, gap), f32)], axis=1)
    spread = spread.astype(bf16)
    left_hi, left_lo = split(mm(twice.astype(bf16), jnp.concatenate([hi, lo], axis=0)))
    wide = ext // 256 * 256
    both = mm(jnp.concatenate([left_hi, left_lo], axis=0), spread[:wide], ((1,), (1,)))
    rest = mm(
        jnp.concatenate([left_hi[wide:], left_lo[wide:]], axis=0), spread[wide:], ((1,), (1,))
    )
    return both[:ext] + both[ext:], rest[: ext - wide] + rest[ext - wide :]


def assemble_kernel(ghost, nodes_any, ham_any, own, halo, raw, ham, left, corner, sem):
    cells = ham.shape[0]
    ext, wide = left.shape
    owned = ext - 2 * ghost
    moves = [(nodes_any, raw)] + [(ham_any.at[c], ham.at[c]) for c in range(cells)]
    copies = [pltpu.make_async_copy(a, b, sem.at[i]) for i, (a, b) in enumerate(moves)]
    for copy in copies:
        copy.start()
    copies[0].wait()
    node = raw[...]
    lower = (node >= owned) & (node < owned + ghost)
    swapped = jnp.where(lower, node + ghost, jnp.where(node >= owned + ghost, node - ghost, node))
    nodes = jnp.where(lax.rem(lax.axis_index("dom"), 2) == 0, swapped, node)
    for c in range(cells):
        copies[1 + c].wait()
        term, rest = cell_term(ham[c], nodes[c : c + 1, :], ext)
        left[...] = term if c == 0 else left[...] + term
        corner[...] = rest if c == 0 else corner[...] + rest
    below = jnp.transpose(left[ext - 128 :, :])[:, 128 - (ext - wide) :]
    right = jnp.concatenate([below, corner[...]], axis=0)
    full = jnp.concatenate([left[...], right], axis=1)
    hi = full.astype(bf16).astype(f32)
    lo = full - hi
    for out, start, stop in ((own, 0, owned), (halo, owned, ext)):
        high = hi[:, start:stop]
        out[...] = jnp.concatenate([high, lo[:, start:stop], high], axis=1).astype(bf16)


def assemble(cell_nodes, cell_ham, ext, ghost):
    cells, n, _ = cell_ham.shape
    wide = ext // 256 * 256
    return pl.pallas_call(
        functools.partial(assemble_kernel, ghost),
        out_shape=(
            shape(ext, 3 * (ext - 2 * ghost), dtype=bf16),
            shape(ext, 6 * ghost, dtype=bf16),
        ),
        in_specs=[pl.BlockSpec(memory_space=pl.ANY)] * 2,
        out_specs=(pl.BlockSpec(memory_space=pltpu.VMEM),) * 2,
        scratch_shapes=[
            pltpu.VMEM((cells, n), jnp.int32),
            pltpu.VMEM((cells, n, n), f32),
            pltpu.VMEM((ext, wide), f32),
            pltpu.VMEM((ext - wide, ext - wide), f32),
            pltpu.SemaphoreType.DMA((1 + cells,)),
        ],
        compiler_params=pltpu.CompilerParams(vmem_limit_bytes=VMEM_MOST),
        cost_estimate=pl.CostEstimate(
            flops=cells * 8 * n * n * ext, bytes_accessed=cells * n * n * 4, transcendentals=0
        ),
    )(cell_nodes, cell_ham)


def own_kernel(v, column, ham, out):
    hi, lo = split(v[...] * column[:, :1])
    out[...] = mm(ham[...], jnp.concatenate([hi, hi, lo], axis=0))


def add_halo(partial, near, far, ham, to_near, to_far):
    ghost = near.shape[0]
    owned = partial.shape[0] - 2 * ghost
    hi, lo = split(jnp.concatenate([near[...], far[...]], axis=0))
    z = partial[...] + mm(ham[...], jnp.concatenate([hi, hi, lo], axis=0))
    to_near[...] = z[owned : owned + ghost]
    to_far[...] = z[owned + ghost :]
    return z[:owned]


def first_kernel(far, partial, near, ham, column, s, base, to_near, to_far):
    z = add_halo(partial, near, far, ham, to_near, to_far)
    base[...] = (sigma_one / filter_half) * (z * column[:, :1] - filter_center * s[...])


def second_kernel(far, partial, near, ham, column, one, s, base, to_near, to_far):
    z = add_halo(partial, near, far, ham, to_near, to_far)
    base[...] = (
        2.0 * sigma_two / filter_half * (z * column[:, :1] - filter_center * one[...])
        - sigma_one * sigma_two * s[...]
    )


def collect(factor, base, from_near, from_far, column, put):
    parts = zip(split_three(from_near[...]), split_three(from_far[...]))
    rows = jnp.concatenate([part for pair in parts for part in pair], axis=0)
    return base[...] + factor * column[:, :1] * mm(put[...], rows)


def middle_kernel(from_far, base, from_near, column, put, pick, one, near_out, far_out):
    filtered = collect(sigma_one / filter_half, base, from_near, from_far, column, put)
    one[...] = filtered
    send_rows(filtered * column[:, :1], pick, near_out, far_out)


def last_kernel(from_far, base, from_near, column, put, two):
    two[...] = collect(2.0 * sigma_two / filter_half, base, from_near, from_far, column, put)


def order_kernel(owner, *refs):
    parts, (hi_out, lo_out) = refs[:-2], refs[-2:]
    here = lax.axis_index("dom")
    for b, part in enumerate(parts):
        slot = here ^ b
        place = jnp.int32(0)
        for p in range(len(parts)):
            place = place + jnp.where(owner[p] == slot, p, 0)
        hi, lo = split(part[...])
        hi_out[place] = hi
        lo_out[place] = lo


def rotated_rows(hi_ref, lo_ref, parts):
    here = lax.axis_index("band")
    total = None
    for r, part in parts:
        k = here ^ r
        hi, lo = split(part)
        rhi, rlo = hi_ref[k], lo_ref[k]
        term = mm(
            jnp.concatenate([hi, lo, hi], axis=1), jnp.concatenate([rhi, rhi, rlo], axis=0)
        )
        total = term if total is None else total + term
    return total


def rotate_kernel(hi_ref, lo_ref, own, one, two, out):
    out[...] = rotated_rows(hi_ref, lo_ref, [(0, own[...]), (1, one[...]), (2, two[...])])


def rotate_last_kernel(hi_ref, lo_ref, total, inner, outer, column, pick, out, near_out, far_out):
    here = lax.axis_index("band")
    third = jnp.where((here == 1) | (here == 2), inner[...], outer[...])
    rows = total[...] + rotated_rows(hi_ref, lo_ref, [(3, third)])
    out[...] = rows
    send_rows(rows * column[:, :1], pick, near_out, far_out)


def flip(count, bits):
    return [(i, i ^ bits) for i in range(count)]


def ordered_rotation(slots, owner, bands):
    rows, cols = slots[0].shape
    total = len(slots) * rows
    hi, lo = call(
        order_kernel,
        (shape(len(slots), rows, cols, dtype=bf16),) * 2,
        [owner, *slots],
        total * cols * 16,
        scalars=(0,),
    )
    return hi.reshape(bands, total // bands, cols), lo.reshape(bands, total // bands, cols)


def shards(states, inv_mass, cell_ham, cell_nodes, send_up, send_down, owner, rotation_store):
    owned, cols = states.shape
    ghost = send_up.shape[0]
    ext = owned + 2 * ghost
    doms, bands = lax.axis_size("dom"), lax.axis_size("band")
    m = inv_mass[None, :]
    up = send_up[None, :]
    dn = send_down[None, :]
    near_pairs = flip(doms, 1)
    far_pairs = [(i, (i - 1 if i % 2 == 0 else i + 1) % doms) for i in range(doms)]
    halo = shape(ghost, cols)
    block = shape(owned, cols)
    small = 4 * ghost * owned * cols * 3

    def exchange(to_near, to_far):
        from_near = lax.ppermute(to_near, "dom", near_pairs)
        from_far = lax.ppermute(to_far, "dom", far_pairs)
        return from_near, from_far

    ham_own, ham_halo = assemble(cell_nodes, cell_ham, ext, ghost)
    column, pick, put = call(
        lists_kernel,
        (
            shape(owned, 128),
            shape(2 * ghost, 3 * owned, dtype=bf16),
            shape(owned, 6 * ghost, dtype=bf16),
        ),
        [m, up, dn],
        owned * owned,
    )
    band = lax.axis_index("band")
    own_columns = lax.dynamic_slice_in_dim(rotation_store, band * cols, cols, 1)
    one = lax.ppermute(states, "band", flip(4, 1))
    two = lax.ppermute(states, "band", flip(4, 2))
    paired = doms == 8 and rotation_store.shape[0] % 16 == 0
    parts = [own_columns]
    if paired:
        parts += [lax.ppermute(own_columns, "dom", flip(doms, b)) for b in (2, 4, 6)]
    ham_own, *parts = lax.optimization_barrier((ham_own, *parts))
    held, one, two, ham_own = lax.optimization_barrier((states, one, two, ham_own))
    inner = lax.ppermute(held, "band", [(0, 0), (1, 2), (2, 1), (3, 3)])
    outer = lax.ppermute(two, "band", flip(4, 1))
    if paired:
        other = [lax.ppermute(part, "dom", near_pairs) for part in parts]
        slots = [part for pair in zip(parts, other) for part in pair]
        rotation = ordered_rotation(slots, owner, bands)
    else:
        columns = lax.all_gather(own_columns, "dom", axis=0, tiled=True)
        columns = columns.reshape(doms, -1, cols)[owner].reshape(bands, -1, cols)
        rotation = split(columns)
    work = 6 * owned * cols * cols
    total = call(rotate_kernel, block, [*rotation, held, one, two], 3 * work)
    turned, to_near, to_far = call(
        rotate_last_kernel,
        (block, halo, halo),
        [*rotation, total, inner, outer, column, pick],
        work,
    )
    wide = shape(ext, cols)
    work = 6 * ext * ext * cols
    near, far = exchange(to_near, to_far)
    partial = call(own_kernel, wide, [turned, column, ham_own], work)
    base, to_near, to_far = call(
        first_kernel,
        (block, halo, halo),
        [far, partial, near, ham_halo, column, turned],
        work,
    )
    near, far = exchange(to_near, to_far)
    filtered, to_near, to_far = call(
        middle_kernel, (block, halo, halo), [far, base, near, column, put, pick], small
    )
    near, far = exchange(to_near, to_far)
    partial = call(own_kernel, wide, [filtered, column, ham_own], work)
    base, to_near, to_far = call(
        second_kernel,
        (block, halo, halo),
        [far, partial, near, ham_halo, column, filtered, turned],
        work,
    )
    near, far = exchange(to_near, to_far)
    return call(last_kernel, block, [far, base, near, column, put], small)


def solution(mesh):
    in_specs = (
        P("dom", "band"),
        P("dom"),
        P("dom", None, None),
        P("dom", None),
        P("dom"),
        P("dom"),
        P(),
        P("dom", None),
    )
    out_specs = P("dom", "band")
    return jax.shard_map(shards, mesh=mesh, in_specs=in_specs, out_specs=out_specs, check_vma=False)
```

```python
import functools

import jax
import jax.numpy as jnp
from jax import lax
from jax.experimental import pallas as pl
from jax.experimental.pallas import tpu as pltpu
from jax.sharding import PartitionSpec as P

filter_center = 2.5
filter_half = 3.5
spectrum_floor = -4.0
sigma_one = filter_half / (spectrum_floor - filter_center)
sigma_two = 1.0 / (2.0 / sigma_one - sigma_one)

f32 = jnp.float32
bf16 = jnp.bfloat16
VMEM_LIMIT = 32 * 1024 * 1024
VMEM_MOST = 56 * 1024 * 1024


def split(x):
    hi = x.astype(bf16)
    lo = (x - hi.astype(f32)).astype(bf16)
    return hi, lo


def mm(a, b, dims=((1,), (0,))):
    return lax.dot_general(a, b, (dims, ((), ())), preferred_element_type=f32)


def select(onehot, x):
    hi, lo = split(x)
    rest = (x - hi.astype(f32) - lo.astype(f32)).astype(bf16)
    return mm(onehot, hi) + mm(onehot, lo) + mm(onehot, rest)


def as_column(row):
    n = row.shape[1]
    here = lax.broadcasted_iota(jnp.int32, (n, n), 0) == lax.broadcasted_iota(jnp.int32, (n, n), 1)
    return jnp.sum(jnp.where(here, row, jnp.zeros_like(row)), axis=1, keepdims=True)


def pick_rows(list_row, owned):
    column = as_column(list_row.astype(f32)).astype(jnp.int32)
    shape = (list_row.shape[1], owned)
    return (lax.broadcasted_iota(jnp.int32, shape, 1) == column).astype(f32).astype(bf16)


def put_rows(list_row, owned):
    shape = (owned, list_row.shape[1])
    return (lax.broadcasted_iota(jnp.int32, shape, 0) == list_row).astype(f32).astype(bf16)


def call(kernel, out_shape, args, cost, scalars=(), **kwargs):
    vmem = pl.BlockSpec(memory_space=pltpu.VMEM)
    smem = pl.BlockSpec(memory_space=pltpu.SMEM)
    specs = [smem if i in scalars else vmem for i in range(len(args))]
    return pl.pallas_call(
        kernel,
        out_shape=out_shape,
        in_specs=specs,
        out_specs=jax.tree.map(lambda _: vmem, out_shape),
        compiler_params=pltpu.CompilerParams(vmem_limit_bytes=VMEM_LIMIT),
        cost_estimate=pl.CostEstimate(flops=cost, bytes_accessed=min(cost, 1 << 20), transcendentals=0),
        **kwargs,
    )(*args)


def shape(*dims, dtype=f32):
    return jax.ShapeDtypeStruct(dims, dtype)


def lists_kernel(m, up, dn, column, pick, put_near, put_far):
    owned = m.shape[1]
    column[...] = jnp.broadcast_to(as_column(m[...]), column.shape)
    even = lax.rem(lax.axis_index("dom"), 2) == 0
    up, dn = up[...], dn[...]
    near, far = jnp.where(even, up, dn), jnp.where(even, dn, up)
    rows = jnp.concatenate([pick_rows(near, owned), pick_rows(far, owned)], axis=0)
    pick[...] = jnp.concatenate([rows.astype(f32)] * 3, axis=1).astype(bf16)
    put_near[...] = jnp.concatenate([put_rows(near, owned).astype(f32)] * 3, axis=1).astype(bf16)
    put_far[...] = jnp.concatenate([put_rows(far, owned).astype(f32)] * 3, axis=1).astype(bf16)


def split_three(x):
    hi, lo = split(x)
    return hi, lo, (x - hi.astype(f32) - lo.astype(f32)).astype(bf16)


def picked(x, pick):
    return mm(pick, jnp.concatenate(split_three(x), axis=0))


def send_rows(x, pick, near_out, far_out):
    rows = picked(x, pick[...])
    ghost = near_out.shape[0]
    near_out[...] = rows[:ghost]
    far_out[...] = rows[ghost:]


def placed(rows, put):
    return mm(put[...], jnp.concatenate(split_three(rows[...]), axis=0))


def cell_term(ham, row, ext):
    n = ham.shape[0]
    gap = -n % 16
    hi, lo = split(jnp.concatenate([ham, jnp.zeros((gap, n), f32)], axis=0))
    spread = lax.broadcasted_iota(jnp.int32, (ext, n), 0) == row
    spread = spread.astype(f32)
    twice = jnp.concatenate([spread, jnp.zeros((ext, gap), f32), spread, jnp.zeros((ext, gap), f32)], axis=1)
    spread = spread.astype(bf16)
    left_hi, left_lo = split(mm(twice.astype(bf16), jnp.concatenate([hi, lo], axis=0)))
    wide = ext // 256 * 256
    both = mm(jnp.concatenate([left_hi, left_lo], axis=0), spread[:wide], ((1,), (1,)))
    rest = mm(
        jnp.concatenate([left_hi[wide:], left_lo[wide:]], axis=0), spread[wide:], ((1,), (1,))
    )
    return both[:ext] + both[ext:], rest[: ext - wide] + rest[ext - wide :]


def assemble_kernel(ghost, nodes_any, ham_any, own, halo, raw, ham, left, corner, sem):
    cells = ham.shape[0]
    ext, wide = left.shape
    owned = ext - 2 * ghost
    moves = [(nodes_any, raw)] + [(ham_any.at[c], ham.at[c]) for c in range(cells)]
    copies = [pltpu.make_async_copy(a, b, sem.at[i]) for i, (a, b) in enumerate(moves)]
    for copy in copies:
        copy.start()
    copies[0].wait()
    node = raw[...]
    lower = (node >= owned) & (node < owned + ghost)
    swapped = jnp.where(lower, node + ghost, jnp.where(node >= owned + ghost, node - ghost, node))
    nodes = jnp.where(lax.rem(lax.axis_index("dom"), 2) == 0, swapped, node)
    for c in range(cells):
        copies[1 + c].wait()
        term, rest = cell_term(ham[c], nodes[c : c + 1, :], ext)
        left[...] = term if c == 0 else left[...] + term
        corner[...] = rest if c == 0 else corner[...] + rest
    below = jnp.transpose(left[ext - 128 :, :])[:, 128 - (ext - wide) :]
    right = jnp.concatenate([below, corner[...]], axis=0)
    full = jnp.concatenate([left[...], right], axis=1)
    hi = full.astype(bf16).astype(f32)
    lo = full - hi
    for out, start, stop in ((own, 0, owned), (halo, owned, ext)):
        high = hi[:, start:stop]
        out[...] = jnp.concatenate([high, lo[:, start:stop], high], axis=1).astype(bf16)


def assemble(cell_nodes, cell_ham, ext, ghost):
    cells, n, _ = cell_ham.shape
    wide = ext // 256 * 256
    return pl.pallas_call(
        functools.partial(assemble_kernel, ghost),
        out_shape=(
            shape(ext, 3 * (ext - 2 * ghost), dtype=bf16),
            shape(ext, 6 * ghost, dtype=bf16),
        ),
        in_specs=[pl.BlockSpec(memory_space=pl.ANY)] * 2,
        out_specs=(pl.BlockSpec(memory_space=pltpu.VMEM),) * 2,
        scratch_shapes=[
            pltpu.VMEM((cells, n), jnp.int32),
            pltpu.VMEM((cells, n, n), f32),
            pltpu.VMEM((ext, wide), f32),
            pltpu.VMEM((ext - wide, ext - wide), f32),
            pltpu.SemaphoreType.DMA((1 + cells,)),
        ],
        compiler_params=pltpu.CompilerParams(vmem_limit_bytes=VMEM_MOST),
        cost_estimate=pl.CostEstimate(
            flops=cells * 8 * n * n * ext, bytes_accessed=cells * n * n * 4, transcendentals=0
        ),
    )(cell_nodes, cell_ham)


def own_kernel(v, column, ham, out):
    hi, lo = split(v[...] * column[:, :1])
    out[...] = mm(ham[...], jnp.concatenate([hi, hi, lo], axis=0))


def add_halo(partial, near, far, ham, to_near, to_far):
    ghost = near.shape[0]
    owned = partial.shape[0] - 2 * ghost
    hi, lo = split(jnp.concatenate([near, far], axis=0))
    z = partial[...] + mm(ham[...], jnp.concatenate([hi, hi, lo], axis=0))
    to_near[...] = z[owned : owned + ghost]
    to_far[...] = z[owned + ghost :]
    return z[:owned]


def first_kernel(far, partial, near, ham, column, s, base, to_near, to_far):
    z = add_halo(partial, near[...], far[...], ham, to_near, to_far)
    base[...] = (sigma_one / filter_half) * (z * column[:, :1] - filter_center * s[...])


def near_sums_kernel(from_near, base, column, put_near, pick, out, to_far):
    scale = column[:, :1]
    rows = base[...] + (sigma_one / filter_half) * scale * placed(from_near, put_near)
    out[...] = rows
    wide = jnp.concatenate([rows * scale, column[...]], axis=1)
    to_far[...] = picked(wide, pick[to_far.shape[0] :, :])


def far_sums_kernel(from_far, base, column, put_far, pick, one, to_near):
    scale = column[:, :1]
    rows = base[...] + (sigma_one / filter_half) * scale * placed(from_far, put_far)
    one[...] = rows
    to_near[...] = picked(rows * scale, pick[: to_near.shape[0], :])


def second_kernel(far, near, sent, partial, ham, column, one, s, base, to_near, to_far):
    cols = sent.shape[1]
    scale = far[:, cols : cols + 1]
    whole = far[:, :cols] + (sigma_one / filter_half) * scale * scale * sent[...]
    z = add_halo(partial, near[...], whole, ham, to_near, to_far)
    base[...] = (
        2.0 * sigma_two / filter_half * (z * column[:, :1] - filter_center * one[...])
        - sigma_one * sigma_two * s[...]
    )


def last_kernel(from_far, base, from_near, column, put_near, put_far, two):
    sums = placed(from_near, put_near) + placed(from_far, put_far)
    two[...] = base[...] + 2.0 * sigma_two / filter_half * column[:, :1] * sums


def order_kernel(owner, *refs):
    parts, (hi_out, lo_out) = refs[:-2], refs[-2:]
    here = lax.axis_index("dom")
    for b, part in enumerate(parts):
        slot = here ^ b
        place = jnp.int32(0)
        for p in range(len(parts)):
            place = place + jnp.where(owner[p] == slot, p, 0)
        hi, lo = split(part[...])
        hi_out[place] = hi
        lo_out[place] = lo


def rotated_rows(hi_ref, lo_ref, parts):
    here = lax.axis_index("band")
    total = None
    for r, part in parts:
        k = here ^ r
        hi, lo = split(part)
        rhi, rlo = hi_ref[k], lo_ref[k]
        term = mm(
            jnp.concatenate([hi, lo, hi], axis=1), jnp.concatenate([rhi, rhi, rlo], axis=0)
        )
        total = term if total is None else total + term
    return total


def rotate_kernel(hi_ref, lo_ref, own, one, two, out):
    out[...] = rotated_rows(hi_ref, lo_ref, [(0, own[...]), (1, one[...]), (2, two[...])])


def rotate_last_kernel(hi_ref, lo_ref, total, inner, outer, column, pick, out, near_out, far_out):
    here = lax.axis_index("band")
    third = jnp.where((here == 1) | (here == 2), inner[...], outer[...])
    rows = total[...] + rotated_rows(hi_ref, lo_ref, [(3, third)])
    out[...] = rows
    send_rows(rows * column[:, :1], pick, near_out, far_out)


def flip(count, bits):
    return [(i, i ^ bits) for i in range(count)]


def ordered_rotation(slots, owner, bands):
    rows, cols = slots[0].shape
    total = len(slots) * rows
    hi, lo = call(
        order_kernel,
        (shape(len(slots), rows, cols, dtype=bf16),) * 2,
        [owner, *slots],
        total * cols * 16,
        scalars=(0,),
    )
    return hi.reshape(bands, total // bands, cols), lo.reshape(bands, total // bands, cols)


def shards(states, inv_mass, cell_ham, cell_nodes, send_up, send_down, owner, rotation_store):
    owned, cols = states.shape
    ghost = send_up.shape[0]
    ext = owned + 2 * ghost
    doms, bands = lax.axis_size("dom"), lax.axis_size("band")
    m = inv_mass[None, :]
    up = send_up[None, :]
    dn = send_down[None, :]
    near_pairs = flip(doms, 1)
    far_pairs = [(i, (i - 1 if i % 2 == 0 else i + 1) % doms) for i in range(doms)]
    halo = shape(ghost, cols)
    block = shape(owned, cols)
    small = 4 * ghost * owned * cols * 3

    def to_pair(rows):
        return lax.ppermute(rows, "dom", near_pairs)

    def to_other(rows):
        return lax.ppermute(rows, "dom", far_pairs)

    ham_own, ham_halo = assemble(cell_nodes, cell_ham, ext, ghost)
    put = shape(owned, 3 * ghost, dtype=bf16)
    column, pick, put_near, put_far = call(
        lists_kernel,
        (shape(owned, 128), shape(2 * ghost, 3 * owned, dtype=bf16), put, put),
        [m, up, dn],
        owned * owned,
    )
    band = lax.axis_index("band")
    own_columns = lax.dynamic_slice_in_dim(rotation_store, band * cols, cols, 1)
    one = lax.ppermute(states, "band", flip(4, 1))
    two = lax.ppermute(states, "band", flip(4, 2))
    paired = doms == 8 and rotation_store.shape[0] % 16 == 0
    parts = [own_columns]
    if paired:
        parts += [lax.ppermute(own_columns, "dom", flip(doms, b)) for b in (2, 4, 6)]
    ham_own, *parts = lax.optimization_barrier((ham_own, *parts))
    held, one, two, ham_own = lax.optimization_barrier((states, one, two, ham_own))
    inner = lax.ppermute(held, "band", [(0, 0), (1, 2), (2, 1), (3, 3)])
    outer = lax.ppermute(two, "band", flip(4, 1))
    if paired:
        other = [lax.ppermute(part, "dom", near_pairs) for part in parts]
        slots = [part for pair in zip(parts, other) for part in pair]
        rotation = ordered_rotation(slots, owner, bands)
    else:
        columns = lax.all_gather(own_columns, "dom", axis=0, tiled=True)
        columns = columns.reshape(doms, -1, cols)[owner].reshape(bands, -1, cols)
        rotation = split(columns)
    work = 6 * owned * cols * cols
    total = call(rotate_kernel, block, [*rotation, held, one, two], 3 * work)
    turned, to_near, to_far = call(
        rotate_last_kernel,
        (block, halo, halo),
        [*rotation, total, inner, outer, column, pick],
        work,
    )
    wide = shape(ext, cols)
    work = 6 * ext * ext * cols
    far, near = to_other(to_far), to_pair(to_near)
    partial = call(own_kernel, wide, [turned, column, ham_own], work)
    base, to_near, sent = call(
        first_kernel,
        (block, halo, halo),
        [far, partial, near, ham_halo, column, turned],
        work,
    )
    from_far, from_near = to_other(sent), to_pair(to_near)
    base, to_far = call(
        near_sums_kernel, (block, shape(ghost, cols + 128)), [from_near, base, column, put_near, pick], small
    )
    far = to_other(to_far)
    filtered, to_near = call(
        far_sums_kernel, (block, halo), [from_far, base, column, put_far, pick], 0
    )
    near = to_pair(to_near)
    partial = call(own_kernel, wide, [filtered, column, ham_own], work)
    base, to_near, to_far = call(
        second_kernel,
        (block, halo, halo),
        [far, near, sent, partial, ham_halo, column, filtered, turned],
        work,
    )
    far, near = to_other(to_far), to_pair(to_near)
    return call(last_kernel, block, [far, base, near, column, put_near, put_far], small)


def solution(mesh):
    in_specs = (
        P("dom", "band"),
        P("dom"),
        P("dom", None, None),
        P("dom", None),
        P("dom"),
        P("dom"),
        P(),
        P("dom", None),
    )
    out_specs = P("dom", "band")
    return jax.shard_map(shards, mesh=mesh, in_specs=in_specs, out_specs=out_specs, check_vma=False)
```

```python
import functools

import jax
import jax.numpy as jnp
from jax import lax
from jax.experimental import pallas as pl
from jax.experimental.pallas import tpu as pltpu
from jax.sharding import PartitionSpec as P

filter_center = 2.5
filter_half = 3.5
spectrum_floor = -4.0
sigma_one = filter_half / (spectrum_floor - filter_center)
sigma_two = 1.0 / (2.0 / sigma_one - sigma_one)

f32 = jnp.float32
bf16 = jnp.bfloat16
VMEM_LIMIT = 32 * 1024 * 1024
VMEM_MOST = 56 * 1024 * 1024


def split(x):
    hi = x.astype(bf16)
    lo = (x - hi.astype(f32)).astype(bf16)
    return hi, lo


def mm(a, b, dims=((1,), (0,))):
    return lax.dot_general(a, b, (dims, ((), ())), preferred_element_type=f32)


def select(onehot, x):
    hi, lo = split(x)
    rest = (x - hi.astype(f32) - lo.astype(f32)).astype(bf16)
    return mm(onehot, hi) + mm(onehot, lo) + mm(onehot, rest)


def as_column(row):
    n = row.shape[1]
    here = lax.broadcasted_iota(jnp.int32, (n, n), 0) == lax.broadcasted_iota(jnp.int32, (n, n), 1)
    return jnp.sum(jnp.where(here, row, jnp.zeros_like(row)), axis=1, keepdims=True)


def pick_rows(list_row, owned):
    column = as_column(list_row.astype(f32)).astype(jnp.int32)
    shape = (list_row.shape[1], owned)
    return (lax.broadcasted_iota(jnp.int32, shape, 1) == column).astype(f32).astype(bf16)


def put_rows(list_row, owned):
    shape = (owned, list_row.shape[1])
    return (lax.broadcasted_iota(jnp.int32, shape, 0) == list_row).astype(f32).astype(bf16)


def call(kernel, out_shape, args, cost, scalars=(), **kwargs):
    vmem = pl.BlockSpec(memory_space=pltpu.VMEM)
    smem = pl.BlockSpec(memory_space=pltpu.SMEM)
    specs = [smem if i in scalars else vmem for i in range(len(args))]
    return pl.pallas_call(
        kernel,
        out_shape=out_shape,
        in_specs=specs,
        out_specs=jax.tree.map(lambda _: vmem, out_shape),
        compiler_params=pltpu.CompilerParams(vmem_limit_bytes=VMEM_LIMIT),
        cost_estimate=pl.CostEstimate(flops=cost, bytes_accessed=min(cost, 1 << 20), transcendentals=0),
        **kwargs,
    )(*args)


def shape(*dims, dtype=f32):
    return jax.ShapeDtypeStruct(dims, dtype)


def lists_kernel(m, up, dn, column, pick, put_near, put_far):
    owned = m.shape[1]
    column[...] = jnp.broadcast_to(as_column(m[...]), column.shape)
    even = lax.rem(lax.axis_index("dom"), 2) == 0
    up, dn = up[...], dn[...]
    near, far = jnp.where(even, up, dn), jnp.where(even, dn, up)
    rows = jnp.concatenate([pick_rows(near, owned), pick_rows(far, owned)], axis=0)
    pick[...] = jnp.concatenate([rows.astype(f32)] * 3, axis=1).astype(bf16)
    put_near[...] = jnp.concatenate([put_rows(near, owned).astype(f32)] * 3, axis=1).astype(bf16)
    put_far[...] = jnp.concatenate([put_rows(far, owned).astype(f32)] * 3, axis=1).astype(bf16)


def split_three(x):
    hi, lo = split(x)
    return hi, lo, (x - hi.astype(f32) - lo.astype(f32)).astype(bf16)


def picked(x, pick):
    return mm(pick, jnp.concatenate(split_three(x), axis=0))


def send_rows(x, pick, near_out, far_out):
    rows = picked(x, pick[...])
    ghost = near_out.shape[0]
    near_out[...] = rows[:ghost]
    far_out[...] = rows[ghost:]


def placed(rows, put):
    return mm(put[...], jnp.concatenate(split_three(rows[...]), axis=0))


def cell_term(ham, row, ext):
    n = ham.shape[0]
    gap = -n % 16
    hi, lo = split(jnp.concatenate([ham, jnp.zeros((gap, n), f32)], axis=0))
    spread = lax.broadcasted_iota(jnp.int32, (ext, n), 0) == row
    spread = spread.astype(f32)
    twice = jnp.concatenate([spread, jnp.zeros((ext, gap), f32), spread, jnp.zeros((ext, gap), f32)], axis=1)
    spread = spread.astype(bf16)
    left_hi, left_lo = split(mm(twice.astype(bf16), jnp.concatenate([hi, lo], axis=0)))
    wide = ext // 256 * 256
    both = mm(jnp.concatenate([left_hi, left_lo], axis=0), spread[:wide], ((1,), (1,)))
    rest = mm(
        jnp.concatenate([left_hi[wide:], left_lo[wide:]], axis=0), spread[wide:], ((1,), (1,))
    )
    return both[:ext] + both[ext:], rest[: ext - wide] + rest[ext - wide :]


def assemble_kernel(ghost, nodes_any, ham_any, own, halo, raw, ham, left, corner, sem):
    cells = ham.shape[0]
    ext, wide = left.shape
    owned = ext - 2 * ghost
    moves = [(nodes_any, raw)] + [(ham_any.at[c], ham.at[c]) for c in range(cells)]
    copies = [pltpu.make_async_copy(a, b, sem.at[i]) for i, (a, b) in enumerate(moves)]
    for copy in copies:
        copy.start()
    copies[0].wait()
    node = raw[...]
    lower = (node >= owned) & (node < owned + ghost)
    swapped = jnp.where(lower, node + ghost, jnp.where(node >= owned + ghost, node - ghost, node))
    nodes = jnp.where(lax.rem(lax.axis_index("dom"), 2) == 0, swapped, node)
    for c in range(cells):
        copies[1 + c].wait()
        term, rest = cell_term(ham[c], nodes[c : c + 1, :], ext)
        left[...] = term if c == 0 else left[...] + term
        corner[...] = rest if c == 0 else corner[...] + rest
    below = jnp.transpose(left[ext - 128 :, :])[:, 128 - (ext - wide) :]
    right = jnp.concatenate([below, corner[...]], axis=0)
    full = jnp.concatenate([left[...], right], axis=1)
    hi = full.astype(bf16).astype(f32)
    lo = full - hi
    for out, start, stop in ((own, 0, owned), (halo, owned, ext)):
        high = hi[:, start:stop]
        out[...] = jnp.concatenate([high, lo[:, start:stop], high], axis=1).astype(bf16)


def assemble(cell_nodes, cell_ham, ext, ghost):
    cells, n, _ = cell_ham.shape
    wide = ext // 256 * 256
    return pl.pallas_call(
        functools.partial(assemble_kernel, ghost),
        out_shape=(
            shape(ext, 3 * (ext - 2 * ghost), dtype=bf16),
            shape(ext, 6 * ghost, dtype=bf16),
        ),
        in_specs=[pl.BlockSpec(memory_space=pl.ANY)] * 2,
        out_specs=(pl.BlockSpec(memory_space=pltpu.VMEM),) * 2,
        scratch_shapes=[
            pltpu.VMEM((cells, n), jnp.int32),
            pltpu.VMEM((cells, n, n), f32),
            pltpu.VMEM((ext, wide), f32),
            pltpu.VMEM((ext - wide, ext - wide), f32),
            pltpu.SemaphoreType.DMA((1 + cells,)),
        ],
        compiler_params=pltpu.CompilerParams(vmem_limit_bytes=VMEM_MOST),
        cost_estimate=pl.CostEstimate(
            flops=cells * 8 * n * n * ext, bytes_accessed=cells * n * n * 4, transcendentals=0
        ),
    )(cell_nodes, cell_ham)


def own_kernel(v, column, ham, out):
    hi, lo = split(v[...] * column[:, :1])
    out[...] = mm(ham[...], jnp.concatenate([hi, hi, lo], axis=0))


def add_halo(partial, near, far, ham, to_near, to_far):
    ghost = near.shape[0]
    owned = partial.shape[0] - 2 * ghost
    hi, lo = split(jnp.concatenate([near, far], axis=0))
    z = partial[...] + mm(ham[...], jnp.concatenate([hi, hi, lo], axis=0))
    to_near[...] = z[owned : owned + ghost]
    to_far[...] = z[owned + ghost :]
    return z[:owned]


def first_kernel(far, partial, near, ham, column, s, base, to_near, to_far):
    z = add_halo(partial, near[...], far[...], ham, to_near, to_far)
    base[...] = (sigma_one / filter_half) * (z * column[:, :1] - filter_center * s[...])


def near_sums_kernel(from_near, base, column, put_near, pick, out, to_far):
    scale = column[:, :1]
    rows = base[...] + (sigma_one / filter_half) * scale * placed(from_near, put_near)
    out[...] = rows
    wide = jnp.concatenate([rows * scale, column[...]], axis=1)
    to_far[...] = picked(wide, pick[to_far.shape[0] :, :])


def far_sums_kernel(from_far, base, column, put_far, pick, one, to_near):
    scale = column[:, :1]
    rows = base[...] + (sigma_one / filter_half) * scale * placed(from_far, put_far)
    one[...] = rows
    to_near[...] = picked(rows * scale, pick[: to_near.shape[0], :])


def second_kernel(far, near, sent, partial, ham, column, one, s, base, to_near, to_far):
    cols = sent.shape[1]
    scale = far[:, cols : cols + 1]
    whole = far[:, :cols] + (sigma_one / filter_half) * scale * scale * sent[...]
    z = add_halo(partial, near[...], whole, ham, to_near, to_far)
    base[...] = (
        2.0 * sigma_two / filter_half * (z * column[:, :1] - filter_center * one[...])
        - sigma_one * sigma_two * s[...]
    )


def last_kernel(from_far, base, from_near, column, put_near, put_far, two):
    sums = placed(from_near, put_near) + placed(from_far, put_far)
    two[...] = base[...] + 2.0 * sigma_two / filter_half * column[:, :1] * sums


def order_kernel(owner, *refs):
    parts, (hi_out, lo_out) = refs[:-2], refs[-2:]
    here = lax.axis_index("dom")
    for b, part in enumerate(parts):
        slot = here ^ b
        place = jnp.int32(0)
        for p in range(len(parts)):
            place = place + jnp.where(owner[p] == slot, p, 0)
        hi, lo = split(part[...])
        hi_out[place] = hi
        lo_out[place] = lo


def rotated_rows(hi_ref, lo_ref, parts):
    here = lax.axis_index("band")
    total = None
    for r, part in parts:
        k = here ^ r
        hi, lo = split(part)
        rhi, rlo = hi_ref[k], lo_ref[k]
        term = mm(
            jnp.concatenate([hi, lo, hi], axis=1), jnp.concatenate([rhi, rhi, rlo], axis=0)
        )
        total = term if total is None else total + term
    return total


def longer_kernel(block, out):
    rows = block.shape[0]
    out[:rows, :] = block[...]
    out[rows:, :] = block[: out.shape[0] - rows, :]


def rotate_kernel(hi_ref, lo_ref, own, one, two, out):
    out[...] = rotated_rows(hi_ref, lo_ref, [(0, own[...]), (1, one[...]), (2, two[...])])


def rotate_last_kernel(hi_ref, lo_ref, total, three, column, pick, out, near_out, far_out):
    rows = total[...] + rotated_rows(hi_ref, lo_ref, [(3, three[: total.shape[0], :])])
    out[...] = rows
    send_rows(rows * column[:, :1], pick, near_out, far_out)


def flip(count, bits):
    return [(i, i ^ bits) for i in range(count)]


def ordered_rotation(slots, owner, bands):
    rows, cols = slots[0].shape
    total = len(slots) * rows
    hi, lo = call(
        order_kernel,
        (shape(len(slots), rows, cols, dtype=bf16),) * 2,
        [owner, *slots],
        0,
        scalars=(0,),
    )
    return hi.reshape(bands, total // bands, cols), lo.reshape(bands, total // bands, cols)


def shards(states, inv_mass, cell_ham, cell_nodes, send_up, send_down, owner, rotation_store):
    owned, cols = states.shape
    ghost = send_up.shape[0]
    ext = owned + 2 * ghost
    doms, bands = lax.axis_size("dom"), lax.axis_size("band")
    m = inv_mass[None, :]
    up = send_up[None, :]
    dn = send_down[None, :]
    near_pairs = flip(doms, 1)
    far_pairs = [(i, (i - 1 if i % 2 == 0 else i + 1) % doms) for i in range(doms)]
    halo = shape(ghost, cols)
    block = shape(owned, cols)
    small = 4 * ghost * owned * cols * 3

    def to_pair(rows):
        return lax.ppermute(rows, "dom", near_pairs)

    def to_other(rows):
        return lax.ppermute(rows, "dom", far_pairs)

    ham_own, ham_halo = assemble(cell_nodes, cell_ham, ext, ghost)
    put = shape(owned, 3 * ghost, dtype=bf16)
    column, pick, put_near, put_far = call(
        lists_kernel,
        (shape(owned, 128), shape(2 * ghost, 3 * owned, dtype=bf16), put, put),
        [m, up, dn],
        owned * owned,
    )
    band = lax.axis_index("band")
    own_columns = lax.dynamic_slice_in_dim(rotation_store, band * cols, cols, 1)
    one = lax.ppermute(states, "band", flip(4, 1))
    two = lax.ppermute(states, "band", flip(4, 2))
    paired = doms == 8 and rotation_store.shape[0] % 16 == 0
    parts = [own_columns]
    if paired:
        parts += [lax.ppermute(own_columns, "dom", flip(doms, b)) for b in (2, 4)]
    ham_own, *parts = lax.optimization_barrier((ham_own, *parts))
    if paired:
        parts.append(lax.ppermute(parts[1], "dom", flip(doms, 4)))
        other = [lax.ppermute(part, "dom", near_pairs) for part in parts[:3]]
    one, two, ham_own = lax.optimization_barrier((one, two, ham_own))
    longer = call(longer_kernel, shape(owned + 8, cols), [two], 0)
    three = lax.ppermute(longer, "band", flip(4, 1))
    if paired:
        two, parts[3] = lax.optimization_barrier((two, parts[3]))
        other.append(lax.ppermute(parts[3], "dom", near_pairs))
        slots = [part for pair in zip(parts, other) for part in pair]
        rotation = ordered_rotation(slots, owner, bands)
    else:
        columns = lax.all_gather(own_columns, "dom", axis=0, tiled=True)
        columns = columns.reshape(doms, -1, cols)[owner].reshape(bands, -1, cols)
        rotation = split(columns)
    work = 6 * owned * cols * cols
    total = call(rotate_kernel, block, [*rotation, states, one, two], 0)
    turned, to_near, to_far = call(
        rotate_last_kernel,
        (block, halo, halo),
        [*rotation, total, three, column, pick],
        work,
    )
    wide = shape(ext, cols)
    work = 6 * ext * ext * cols
    far, near = to_other(to_far), to_pair(to_near)
    partial = call(own_kernel, wide, [turned, column, ham_own], work)
    base, to_near, sent = call(
        first_kernel,
        (block, halo, halo),
        [far, partial, near, ham_halo, column, turned],
        work,
    )
    from_far, from_near = to_other(sent), to_pair(to_near)
    base, to_far = call(
        near_sums_kernel, (block, shape(ghost, cols + 128)), [from_near, base, column, put_near, pick], small
    )
    far = to_other(to_far)
    filtered, to_near = call(
        far_sums_kernel, (block, halo), [from_far, base, column, put_far, pick], 0
    )
    near = to_pair(to_near)
    partial = call(own_kernel, wide, [filtered, column, ham_own], work)
    base, to_near, to_far = call(
        second_kernel,
        (block, halo, halo),
        [far, near, sent, partial, ham_halo, column, filtered, turned],
        work,
    )
    far, near = to_other(to_far), to_pair(to_near)
    return call(last_kernel, block, [far, base, near, column, put_near, put_far], small)


def solution(mesh):
    in_specs = (
        P("dom", "band"),
        P("dom"),
        P("dom", None, None),
        P("dom", None),
        P("dom"),
        P("dom"),
        P(),
        P("dom", None),
    )
    out_specs = P("dom", "band")
    return jax.shard_map(shards, mesh=mesh, in_specs=in_specs, out_specs=out_specs, check_vma=False)
```

```python
import functools

import jax
import jax.numpy as jnp
from jax import lax
from jax.experimental import pallas as pl
from jax.experimental.pallas import tpu as pltpu
from jax.sharding import PartitionSpec as P

filter_center = 2.5
filter_half = 3.5
spectrum_floor = -4.0
sigma_one = filter_half / (spectrum_floor - filter_center)
sigma_two = 1.0 / (2.0 / sigma_one - sigma_one)

f32 = jnp.float32
bf16 = jnp.bfloat16
VMEM_LIMIT = 32 * 1024 * 1024
VMEM_MOST = 56 * 1024 * 1024


def split(x):
    hi = x.astype(bf16)
    lo = (x - hi.astype(f32)).astype(bf16)
    return hi, lo


def mm(a, b, dims=((1,), (0,))):
    return lax.dot_general(a, b, (dims, ((), ())), preferred_element_type=f32)


def select(onehot, x):
    hi, lo = split(x)
    rest = (x - hi.astype(f32) - lo.astype(f32)).astype(bf16)
    return mm(onehot, hi) + mm(onehot, lo) + mm(onehot, rest)


def as_column(row):
    n = row.shape[1]
    here = lax.broadcasted_iota(jnp.int32, (n, n), 0) == lax.broadcasted_iota(jnp.int32, (n, n), 1)
    return jnp.sum(jnp.where(here, row, jnp.zeros_like(row)), axis=1, keepdims=True)


def pick_rows(list_row, owned):
    column = as_column(list_row.astype(f32)).astype(jnp.int32)
    shape = (list_row.shape[1], owned)
    return (lax.broadcasted_iota(jnp.int32, shape, 1) == column).astype(f32).astype(bf16)


def put_rows(list_row, owned):
    shape = (owned, list_row.shape[1])
    return (lax.broadcasted_iota(jnp.int32, shape, 0) == list_row).astype(f32).astype(bf16)


def call(kernel, out_shape, args, cost, scalars=(), **kwargs):
    vmem = pl.BlockSpec(memory_space=pltpu.VMEM)
    smem = pl.BlockSpec(memory_space=pltpu.SMEM)
    specs = [smem if i in scalars else vmem for i in range(len(args))]
    return pl.pallas_call(
        kernel,
        out_shape=out_shape,
        in_specs=specs,
        out_specs=jax.tree.map(lambda _: vmem, out_shape),
        compiler_params=pltpu.CompilerParams(vmem_limit_bytes=VMEM_LIMIT),
        cost_estimate=pl.CostEstimate(flops=cost, bytes_accessed=min(cost, 1 << 20), transcendentals=0),
        **kwargs,
    )(*args)


def shape(*dims, dtype=f32):
    return jax.ShapeDtypeStruct(dims, dtype)


def lists_kernel(m, up, dn, column, pick, put_near, put_far):
    owned = m.shape[1]
    column[...] = jnp.broadcast_to(as_column(m[...]), column.shape)
    even = lax.rem(lax.axis_index("dom"), 2) == 0
    up, dn = up[...], dn[...]
    near, far = jnp.where(even, up, dn), jnp.where(even, dn, up)
    rows = jnp.concatenate([pick_rows(near, owned), pick_rows(far, owned)], axis=0)
    pick[...] = jnp.concatenate([rows.astype(f32)] * 3, axis=1).astype(bf16)
    put_near[...] = jnp.concatenate([put_rows(near, owned).astype(f32)] * 3, axis=1).astype(bf16)
    put_far[...] = jnp.concatenate([put_rows(far, owned).astype(f32)] * 3, axis=1).astype(bf16)


def split_three(x):
    hi, lo = split(x)
    return hi, lo, (x - hi.astype(f32) - lo.astype(f32)).astype(bf16)


def picked(x, pick):
    return mm(pick, jnp.concatenate(split_three(x), axis=0))


def send_rows(x, pick, near_out, far_out):
    rows = picked(x, pick[...])
    ghost = near_out.shape[0]
    near_out[...] = rows[:ghost]
    far_out[...] = rows[ghost:]


def placed(rows, put):
    return mm(put[...], jnp.concatenate(split_three(rows[...]), axis=0))


def cell_term(ham, row, ext):
    n = ham.shape[0]
    gap = -n % 16
    hi, lo = split(jnp.concatenate([ham, jnp.zeros((gap, n), f32)], axis=0))
    spread = lax.broadcasted_iota(jnp.int32, (ext, n), 0) == row
    spread = spread.astype(f32)
    twice = jnp.concatenate([spread, jnp.zeros((ext, gap), f32), spread, jnp.zeros((ext, gap), f32)], axis=1)
    spread = spread.astype(bf16)
    left_hi, left_lo = split(mm(twice.astype(bf16), jnp.concatenate([hi, lo], axis=0)))
    wide = ext // 256 * 256
    both = mm(jnp.concatenate([left_hi, left_lo], axis=0), spread[:wide], ((1,), (1,)))
    rest = mm(
        jnp.concatenate([left_hi[wide:], left_lo[wide:]], axis=0), spread[wide:], ((1,), (1,))
    )
    return both[:ext] + both[ext:], rest[: ext - wide] + rest[ext - wide :]


def assemble_kernel(ghost, nodes_any, ham_any, own, halo, raw, ham, left, corner, sem):
    cells = ham.shape[0]
    ext, wide = left.shape
    owned = ext - 2 * ghost
    moves = [(nodes_any, raw)] + [(ham_any.at[c], ham.at[c]) for c in range(cells)]
    copies = [pltpu.make_async_copy(a, b, sem.at[i]) for i, (a, b) in enumerate(moves)]
    for copy in copies:
        copy.start()
    copies[0].wait()
    node = raw[...]
    lower = (node >= owned) & (node < owned + ghost)
    swapped = jnp.where(lower, node + ghost, jnp.where(node >= owned + ghost, node - ghost, node))
    nodes = jnp.where(lax.rem(lax.axis_index("dom"), 2) == 0, swapped, node)
    for c in range(cells):
        copies[1 + c].wait()
        term, rest = cell_term(ham[c], nodes[c : c + 1, :], ext)
        left[...] = term if c == 0 else left[...] + term
        corner[...] = rest if c == 0 else corner[...] + rest
    below = jnp.transpose(left[ext - 128 :, :])[:, 128 - (ext - wide) :]
    right = jnp.concatenate([below, corner[...]], axis=0)
    full = jnp.concatenate([left[...], right], axis=1)
    hi = full.astype(bf16).astype(f32)
    lo = full - hi
    for out, start, stop in ((own, 0, owned), (halo, owned, ext)):
        high = hi[:, start:stop]
        out[...] = jnp.concatenate([high, lo[:, start:stop], high], axis=1).astype(bf16)


def assemble(cell_nodes, cell_ham, ext, ghost):
    cells, n, _ = cell_ham.shape
    wide = ext // 256 * 256
    return pl.pallas_call(
        functools.partial(assemble_kernel, ghost),
        out_shape=(
            shape(ext, 3 * (ext - 2 * ghost), dtype=bf16),
            shape(ext, 6 * ghost, dtype=bf16),
        ),
        in_specs=[pl.BlockSpec(memory_space=pl.ANY)] * 2,
        out_specs=(pl.BlockSpec(memory_space=pltpu.VMEM),) * 2,
        scratch_shapes=[
            pltpu.VMEM((cells, n), jnp.int32),
            pltpu.VMEM((cells, n, n), f32),
            pltpu.VMEM((ext, wide), f32),
            pltpu.VMEM((ext - wide, ext - wide), f32),
            pltpu.SemaphoreType.DMA((1 + cells,)),
        ],
        compiler_params=pltpu.CompilerParams(vmem_limit_bytes=VMEM_MOST),
        cost_estimate=pl.CostEstimate(
            flops=cells * 8 * n * n * ext, bytes_accessed=cells * n * n * 4, transcendentals=0
        ),
    )(cell_nodes, cell_ham)


def own_kernel(v, column, ham, out):
    hi, lo = split(v[...] * column[:, :1])
    out[...] = mm(ham[...], jnp.concatenate([hi, hi, lo], axis=0))


def add_halo(partial, near, far, ham, to_near, to_far):
    ghost = near.shape[0]
    owned = partial.shape[0] - 2 * ghost
    hi, lo = split(jnp.concatenate([near, far], axis=0))
    z = partial[...] + mm(ham[...], jnp.concatenate([hi, hi, lo], axis=0))
    to_near[...] = z[owned : owned + ghost]
    to_far[...] = z[owned + ghost :]
    return z[:owned]


def first_kernel(far, partial, near, ham, column, s, base, to_near, to_far):
    z = add_halo(partial, near[...], far[...], ham, to_near, to_far)
    base[...] = (sigma_one / filter_half) * (z * column[:, :1] - filter_center * s[...])


def near_sums_kernel(from_near, base, column, put_near, pick, out, to_far):
    scale = column[:, :1]
    rows = base[...] + (sigma_one / filter_half) * scale * placed(from_near, put_near)
    out[...] = rows
    wide = jnp.concatenate([rows * scale, column[...]], axis=1)
    to_far[...] = picked(wide, pick[to_far.shape[0] :, :])


def far_sums_kernel(from_far, base, column, put_far, pick, one, to_near):
    scale = column[:, :1]
    rows = base[...] + (sigma_one / filter_half) * scale * placed(from_far, put_far)
    one[...] = rows
    to_near[...] = picked(rows * scale, pick[: to_near.shape[0], :])


def second_kernel(far, near, sent, partial, ham, column, one, s, base, to_near, to_far):
    cols = sent.shape[1]
    scale = far[:, cols : cols + 1]
    whole = far[:, :cols] + (sigma_one / filter_half) * scale * scale * sent[...]
    z = add_halo(partial, near[...], whole, ham, to_near, to_far)
    base[...] = (
        2.0 * sigma_two / filter_half * (z * column[:, :1] - filter_center * one[...])
        - sigma_one * sigma_two * s[...]
    )


def last_kernel(from_far, base, from_near, column, put_near, put_far, two):
    sums = placed(from_near, put_near) + placed(from_far, put_far)
    two[...] = base[...] + 2.0 * sigma_two / filter_half * column[:, :1] * sums


def order_kernel(owner, *refs):
    parts, (hi_out, lo_out) = refs[:-2], refs[-2:]
    here = lax.axis_index("dom")
    for b, part in enumerate(parts):
        slot = here ^ b
        place = jnp.int32(0)
        for p in range(len(parts)):
            place = place + jnp.where(owner[p] == slot, p, 0)
        hi, lo = split(part[...])
        hi_out[place] = hi
        lo_out[place] = lo


def rotated_rows(hi_ref, lo_ref, parts):
    here = lax.axis_index("band")
    total = None
    for r, part in parts:
        k = here ^ r
        hi, lo = split(part)
        rhi, rlo = hi_ref[k], lo_ref[k]
        term = mm(
            jnp.concatenate([hi, lo, hi], axis=1), jnp.concatenate([rhi, rhi, rlo], axis=0)
        )
        total = term if total is None else total + term
    return total


def longer_kernel(block, out):
    rows = block.shape[0]
    out[:rows, :] = block[...]
    out[rows:, :] = block[: out.shape[0] - rows, :]


def rotate_kernel(hi_ref, lo_ref, own, one, two, out):
    out[...] = rotated_rows(hi_ref, lo_ref, [(0, own[...]), (1, one[...]), (2, two[...])])


def rotate_last_kernel(hi_ref, lo_ref, total, three, column, pick, out, near_out, far_out):
    rows = total[...] + rotated_rows(hi_ref, lo_ref, [(3, three[: total.shape[0], :])])
    out[...] = rows
    send_rows(rows * column[:, :1], pick, near_out, far_out)


def flip(count, bits):
    return [(i, i ^ bits) for i in range(count)]


def ordered_rotation(slots, owner, bands):
    rows, cols = slots[0].shape
    total = len(slots) * rows
    hi, lo = call(
        order_kernel,
        (shape(len(slots), rows, cols, dtype=bf16),) * 2,
        [owner, *slots],
        0,
        scalars=(0,),
    )
    return hi.reshape(bands, total // bands, cols), lo.reshape(bands, total // bands, cols)


def shards(states, inv_mass, cell_ham, cell_nodes, send_up, send_down, owner, rotation_store):
    owned, cols = states.shape
    ghost = send_up.shape[0]
    ext = owned + 2 * ghost
    doms, bands = lax.axis_size("dom"), lax.axis_size("band")
    m = inv_mass[None, :]
    up = send_up[None, :]
    dn = send_down[None, :]
    near_pairs = flip(doms, 1)
    far_pairs = [(i, (i - 1 if i % 2 == 0 else i + 1) % doms) for i in range(doms)]
    halo = shape(ghost, cols)
    block = shape(owned, cols)
    small = 4 * ghost * owned * cols * 3

    def to_pair(rows):
        return lax.ppermute(rows, "dom", near_pairs)

    def to_other(rows):
        return lax.ppermute(rows, "dom", far_pairs)

    ham_own, ham_halo = assemble(cell_nodes, cell_ham, ext, ghost)
    put = shape(owned, 3 * ghost, dtype=bf16)
    column, pick, put_near, put_far = call(
        lists_kernel,
        (shape(owned, 128), shape(2 * ghost, 3 * owned, dtype=bf16), put, put),
        [m, up, dn],
        owned * owned,
    )
    band = lax.axis_index("band")
    own_columns = lax.dynamic_slice_in_dim(rotation_store, band * cols, cols, 1)
    one = lax.ppermute(states, "band", flip(4, 1))
    two = lax.ppermute(states, "band", flip(4, 2))
    paired = doms == 8 and rotation_store.shape[0] % 16 == 0
    parts = [own_columns]
    if paired:
        parts += [lax.ppermute(own_columns, "dom", flip(doms, b)) for b in (2, 4, 6)]
    one, two, ham_own = lax.optimization_barrier((one, two, ham_own))
    longer = call(longer_kernel, shape(owned + 8, cols), [two], 0)
    three = lax.ppermute(longer, "band", flip(4, 1))
    two, *parts = lax.optimization_barrier((two, *parts))
    if paired:
        other = [lax.ppermute(part, "dom", near_pairs) for part in parts]
        slots = [part for pair in zip(parts, other) for part in pair]
        rotation = ordered_rotation(slots, owner, bands)
    else:
        columns = lax.all_gather(own_columns, "dom", axis=0, tiled=True)
        columns = columns.reshape(doms, -1, cols)[owner].reshape(bands, -1, cols)
        rotation = split(columns)
    work = 6 * owned * cols * cols
    total = call(rotate_kernel, block, [*rotation, states, one, two], 0)
    turned, to_near, to_far = call(
        rotate_last_kernel,
        (block, halo, halo),
        [*rotation, total, three, column, pick],
        work,
    )
    wide = shape(ext, cols)
    work = 6 * ext * ext * cols
    far, near = to_other(to_far), to_pair(to_near)
    partial = call(own_kernel, wide, [turned, column, ham_own], work)
    base, to_near, sent = call(
        first_kernel,
        (block, halo, halo),
        [far, partial, near, ham_halo, column, turned],
        work,
    )
    from_far, from_near = to_other(sent), to_pair(to_near)
    base, to_far = call(
        near_sums_kernel, (block, shape(ghost, cols + 128)), [from_near, base, column, put_near, pick], 0
    )
    far = to_other(to_far)
    filtered, to_near = call(
        far_sums_kernel, (block, halo), [from_far, base, column, put_far, pick], 0
    )
    near = to_pair(to_near)
    partial = call(own_kernel, wide, [filtered, column, ham_own], work)
    base, to_near, to_far = call(
        second_kernel,
        (block, halo, halo),
        [far, near, sent, partial, ham_halo, column, filtered, turned],
        work,
    )
    far, near = to_other(to_far), to_pair(to_near)
    return call(last_kernel, block, [far, base, near, column, put_near, put_far], small)


def solution(mesh):
    in_specs = (
        P("dom", "band"),
        P("dom"),
        P("dom", None, None),
        P("dom", None),
        P("dom"),
        P("dom"),
        P(),
        P("dom", None),
    )
    out_specs = P("dom", "band")
    return jax.shard_map(shards, mesh=mesh, in_specs=in_specs, out_specs=out_specs, check_vma=False)
```

```python
import functools

import jax
import jax.numpy as jnp
from jax import lax
from jax.experimental import pallas as pl
from jax.experimental.pallas import tpu as pltpu
from jax.sharding import PartitionSpec as P

filter_center = 2.5
filter_half = 3.5
spectrum_floor = -4.0
sigma_one = filter_half / (spectrum_floor - filter_center)
sigma_two = 1.0 / (2.0 / sigma_one - sigma_one)

f32 = jnp.float32
bf16 = jnp.bfloat16
VMEM_LIMIT = 32 * 1024 * 1024
VMEM_MOST = 56 * 1024 * 1024


def split(x):
    hi = x.astype(bf16)
    lo = (x - hi.astype(f32)).astype(bf16)
    return hi, lo


def mm(a, b, dims=((1,), (0,))):
    return lax.dot_general(a, b, (dims, ((), ())), preferred_element_type=f32)


def select(onehot, x):
    hi, lo = split(x)
    rest = (x - hi.astype(f32) - lo.astype(f32)).astype(bf16)
    return mm(onehot, hi) + mm(onehot, lo) + mm(onehot, rest)


def as_column(row):
    n = row.shape[1]
    here = lax.broadcasted_iota(jnp.int32, (n, n), 0) == lax.broadcasted_iota(jnp.int32, (n, n), 1)
    return jnp.sum(jnp.where(here, row, jnp.zeros_like(row)), axis=1, keepdims=True)


def pick_rows(list_row, owned):
    column = as_column(list_row.astype(f32)).astype(jnp.int32)
    shape = (list_row.shape[1], owned)
    return (lax.broadcasted_iota(jnp.int32, shape, 1) == column).astype(f32).astype(bf16)


def put_rows(list_row, owned):
    shape = (owned, list_row.shape[1])
    return (lax.broadcasted_iota(jnp.int32, shape, 0) == list_row).astype(f32).astype(bf16)


def call(kernel, out_shape, args, cost, scalars=(), **kwargs):
    vmem = pl.BlockSpec(memory_space=pltpu.VMEM)
    smem = pl.BlockSpec(memory_space=pltpu.SMEM)
    specs = [smem if i in scalars else vmem for i in range(len(args))]
    return pl.pallas_call(
        kernel,
        out_shape=out_shape,
        in_specs=specs,
        out_specs=jax.tree.map(lambda _: vmem, out_shape),
        compiler_params=pltpu.CompilerParams(vmem_limit_bytes=VMEM_LIMIT),
        cost_estimate=pl.CostEstimate(flops=cost, bytes_accessed=min(cost, 1 << 20), transcendentals=0),
        **kwargs,
    )(*args)


def shape(*dims, dtype=f32):
    return jax.ShapeDtypeStruct(dims, dtype)


def lists_kernel(m, up, dn, column, pick, put_near, put_far, far_is_near, near_is_far, scales):
    owned = m.shape[1]
    column[...] = jnp.broadcast_to(as_column(m[...]), column.shape)
    even = lax.rem(lax.axis_index("dom"), 2) == 0
    up, dn = up[...], dn[...]
    near, far = jnp.where(even, up, dn), jnp.where(even, dn, up)
    rows = jnp.concatenate([pick_rows(near, owned), pick_rows(far, owned)], axis=0)
    pick[...] = jnp.concatenate([rows.astype(f32)] * 3, axis=1).astype(bf16)
    put_near[...] = jnp.concatenate([put_rows(near, owned).astype(f32)] * 3, axis=1).astype(bf16)
    put_far[...] = jnp.concatenate([put_rows(far, owned).astype(f32)] * 3, axis=1).astype(bf16)
    for out, these, those in ((far_is_near, far, near), (near_is_far, near, far)):
        same = as_column(these.astype(f32)) == those.astype(f32)
        out[...] = jnp.concatenate([same.astype(f32)] * 3, axis=1).astype(bf16)
    scales[...] = picked(column[...], pick[...])


def split_three(x):
    hi, lo = split(x)
    return hi, lo, (x - hi.astype(f32) - lo.astype(f32)).astype(bf16)


def picked(x, pick):
    return mm(pick, jnp.concatenate(split_three(x), axis=0))


def send_rows(x, pick, near_out, far_out):
    rows = picked(x, pick[...])
    ghost = near_out.shape[0]
    near_out[...] = rows[:ghost]
    far_out[...] = rows[ghost:]


def placed(rows, put):
    return mm(put[...], jnp.concatenate(split_three(rows[...]), axis=0))


def cell_term(ham, row, ext):
    n = ham.shape[0]
    gap = -n % 16
    hi, lo = split(jnp.concatenate([ham, jnp.zeros((gap, n), f32)], axis=0))
    spread = lax.broadcasted_iota(jnp.int32, (ext, n), 0) == row
    spread = spread.astype(f32)
    twice = jnp.concatenate([spread, jnp.zeros((ext, gap), f32), spread, jnp.zeros((ext, gap), f32)], axis=1)
    spread = spread.astype(bf16)
    left_hi, left_lo = split(mm(twice.astype(bf16), jnp.concatenate([hi, lo], axis=0)))
    wide = ext // 256 * 256
    both = mm(jnp.concatenate([left_hi, left_lo], axis=0), spread[:wide], ((1,), (1,)))
    rest = mm(
        jnp.concatenate([left_hi[wide:], left_lo[wide:]], axis=0), spread[wide:], ((1,), (1,))
    )
    return both[:ext] + both[ext:], rest[: ext - wide] + rest[ext - wide :]


def assemble_kernel(ghost, nodes_any, ham_any, own, halo, raw, ham, left, corner, sem):
    cells = ham.shape[0]
    ext, wide = left.shape
    owned = ext - 2 * ghost
    moves = [(nodes_any, raw)] + [(ham_any.at[c], ham.at[c]) for c in range(cells)]
    copies = [pltpu.make_async_copy(a, b, sem.at[i]) for i, (a, b) in enumerate(moves)]
    for copy in copies:
        copy.start()
    copies[0].wait()
    node = raw[...]
    lower = (node >= owned) & (node < owned + ghost)
    swapped = jnp.where(lower, node + ghost, jnp.where(node >= owned + ghost, node - ghost, node))
    nodes = jnp.where(lax.rem(lax.axis_index("dom"), 2) == 0, swapped, node)
    for c in range(cells):
        copies[1 + c].wait()
        term, rest = cell_term(ham[c], nodes[c : c + 1, :], ext)
        left[...] = term if c == 0 else left[...] + term
        corner[...] = rest if c == 0 else corner[...] + rest
    below = jnp.transpose(left[ext - 128 :, :])[:, 128 - (ext - wide) :]
    right = jnp.concatenate([below, corner[...]], axis=0)
    full = jnp.concatenate([left[...], right], axis=1)
    hi = full.astype(bf16).astype(f32)
    lo = full - hi
    for out, start, stop in ((own, 0, owned), (halo, owned, ext)):
        high = hi[:, start:stop]
        out[...] = jnp.concatenate([high, lo[:, start:stop], high], axis=1).astype(bf16)


def assemble(cell_nodes, cell_ham, ext, ghost):
    cells, n, _ = cell_ham.shape
    wide = ext // 256 * 256
    return pl.pallas_call(
        functools.partial(assemble_kernel, ghost),
        out_shape=(
            shape(ext, 3 * (ext - 2 * ghost), dtype=bf16),
            shape(ext, 6 * ghost, dtype=bf16),
        ),
        in_specs=[pl.BlockSpec(memory_space=pl.ANY)] * 2,
        out_specs=(pl.BlockSpec(memory_space=pltpu.VMEM),) * 2,
        scratch_shapes=[
            pltpu.VMEM((cells, n), jnp.int32),
            pltpu.VMEM((cells, n, n), f32),
            pltpu.VMEM((ext, wide), f32),
            pltpu.VMEM((ext - wide, ext - wide), f32),
            pltpu.SemaphoreType.DMA((1 + cells,)),
        ],
        compiler_params=pltpu.CompilerParams(vmem_limit_bytes=VMEM_MOST),
        cost_estimate=pl.CostEstimate(
            flops=cells * 8 * n * n * ext, bytes_accessed=cells * n * n * 4, transcendentals=0
        ),
    )(cell_nodes, cell_ham)


def own_kernel(v, column, ham, out):
    hi, lo = split(v[...] * column[:, :1])
    out[...] = mm(ham[...], jnp.concatenate([hi, hi, lo], axis=0))


def halo_part(near, far, ham):
    hi, lo = split(jnp.concatenate([near, far], axis=0))
    return mm(ham, jnp.concatenate([hi, hi, lo], axis=0))


def completed(far, sent):
    cols = sent.shape[1]
    scale = far[:, cols : cols + 1]
    return far[:, :cols] + (sigma_one / filter_half) * scale * scale * sent[...]


def send_ham_kernel(ham, pick, out):
    halo, owned = out.shape[0] * 2 // 3, pick.shape[1] // 3
    ghost = halo // 2
    out[:halo, :] = ham[owned:, :]
    out[halo:, :] = mm(pick[ghost:, :owned], ham[:owned, :]).astype(bf16)


def first_partial_kernel(v, column, ham, pick, out, far_out):
    own_kernel(v, column, ham, out)
    ghost = far_out.shape[0]
    far_out[...] = picked(out[: v.shape[0], :], pick[ghost:, :])


def first_sums_kernel(
    far, near, partial, far_partial, far_sent, ham, scales, to_near, to_far, far_rows
):
    ghost = near.shape[0]
    owned = partial.shape[0] - 2 * ghost
    z = halo_part(near[...], far[...], ham[...])
    to_near[...] = partial[owned : owned + ghost, :] + z[:ghost]
    to_far[...] = partial[owned + ghost :, :] + z[ghost : 2 * ghost]
    scale = scales[ghost:, :1]
    rows = scale * scale * (far_partial[...] + z[2 * ghost :])
    far_rows[...] = (sigma_one / filter_half) * (rows - filter_center * far_sent[...])


def first_own_kernel(far, near, partial, ham, column, s, base):
    owned = s.shape[0]
    z = partial[:owned, :] + halo_part(near[...], far[...], ham[:owned, :])
    base[...] = (sigma_one / filter_half) * (z * column[:, :1] - filter_center * s[...])


def far_rows_kernel(from_near, far_rows, far_is_near, scales, out):
    ghost, cols = far_rows.shape
    scale = scales[ghost:, :]
    added = (sigma_one / filter_half) * scale[:, :1] * scale[:, :1] * placed(from_near, far_is_near)
    out[...] = jnp.concatenate([far_rows[...] + added, scale], axis=1)


def near_sums_kernel(from_near, base, column, put_near, pick, out, near_rows):
    scale = column[:, :1]
    rows = base[...] + (sigma_one / filter_half) * scale * placed(from_near, put_near)
    out[...] = rows
    near_rows[...] = picked(rows * scale, pick[: near_rows.shape[0], :])


def near_rows_kernel(from_far, near_rows, near_is_far, scales, out):
    scale = scales[: out.shape[0], :1]
    added = (sigma_one / filter_half) * scale * scale * placed(from_far, near_is_far)
    out[...] = near_rows[...] + added


def far_sums_kernel(from_far, base, column, put_far, one):
    scale = (sigma_one / filter_half) * column[:, :1]
    one[...] = base[...] + scale * placed(from_far, put_far)


def second_sums_kernel(far, near, sent, partial, ham, to_near, to_far):
    ghost = near.shape[0]
    owned = partial.shape[0] - 2 * ghost
    z = partial[owned:, :] + halo_part(near[...], completed(far, sent), ham[owned:, :])
    to_near[...] = z[:ghost]
    to_far[...] = z[ghost:]


def second_own_kernel(far, near, sent, partial, ham, column, one, s, base):
    owned = s.shape[0]
    z = partial[:owned, :] + halo_part(near[...], completed(far, sent), ham[:owned, :])
    base[...] = (
        2.0 * sigma_two / filter_half * (z * column[:, :1] - filter_center * one[...])
        - sigma_one * sigma_two * s[...]
    )


def last_kernel(from_far, base, from_near, column, put_near, put_far, out):
    sums = placed(from_near, put_near) + placed(from_far, put_far)
    out[...] = base[...] + 2.0 * sigma_two / filter_half * column[:, :1] * sums


def order_kernel(owner, *refs):
    parts, (hi_out, lo_out) = refs[:-2], refs[-2:]
    here = lax.axis_index("dom")
    for b, part in enumerate(parts):
        slot = here ^ b
        place = jnp.int32(0)
        for p in range(len(parts)):
            place = place + jnp.where(owner[p] == slot, p, 0)
        hi, lo = split(part[...])
        hi_out[place] = hi
        lo_out[place] = lo


def rotated_rows(hi_ref, lo_ref, parts):
    here = lax.axis_index("band")
    total = None
    for r, part in parts:
        k = here ^ r
        hi, lo = split(part)
        rhi, rlo = hi_ref[k], lo_ref[k]
        term = mm(
            jnp.concatenate([hi, lo, hi], axis=1), jnp.concatenate([rhi, rhi, rlo], axis=0)
        )
        total = term if total is None else total + term
    return total


def longer_kernel(block, out):
    rows = block.shape[0]
    out[:rows, :] = block[...]
    out[rows:, :] = block[: out.shape[0] - rows, :]


def rotate_kernel(hi_ref, lo_ref, own, one, two, out):
    out[...] = rotated_rows(hi_ref, lo_ref, [(0, own[...]), (1, one[...]), (2, two[...])])


def rotate_last_kernel(hi_ref, lo_ref, total, three, column, pick, out, near_out, far_out):
    rows = total[...] + rotated_rows(hi_ref, lo_ref, [(3, three[: total.shape[0], :])])
    out[...] = rows
    send_rows(rows * column[:, :1], pick, near_out, far_out)


def flip(count, bits):
    return [(i, i ^ bits) for i in range(count)]


def ordered_rotation(slots, owner, bands):
    rows, cols = slots[0].shape
    total = len(slots) * rows
    hi, lo = call(
        order_kernel,
        (shape(len(slots), rows, cols, dtype=bf16),) * 2,
        [owner, *slots],
        0,
        scalars=(0,),
    )
    return hi.reshape(bands, total // bands, cols), lo.reshape(bands, total // bands, cols)


def shards(states, inv_mass, cell_ham, cell_nodes, send_up, send_down, owner, rotation_store):
    owned, cols = states.shape
    ghost = send_up.shape[0]
    ext = owned + 2 * ghost
    doms, bands = lax.axis_size("dom"), lax.axis_size("band")
    m = inv_mass[None, :]
    up = send_up[None, :]
    dn = send_down[None, :]
    near_pairs = flip(doms, 1)
    far_pairs = [(i, (i - 1 if i % 2 == 0 else i + 1) % doms) for i in range(doms)]
    halo = shape(ghost, cols)
    block = shape(owned, cols)
    small = 4 * ghost * owned * cols * 3

    def to_pair(rows):
        return lax.ppermute(rows, "dom", near_pairs)

    def to_other(rows):
        return lax.ppermute(rows, "dom", far_pairs)

    ham_own, ham_halo = assemble(cell_nodes, cell_ham, ext, ghost)
    put = shape(owned, 3 * ghost, dtype=bf16)
    cross = shape(ghost, 3 * ghost, dtype=bf16)
    column, pick, put_near, put_far, far_is_near, near_is_far, scales = call(
        lists_kernel,
        (
            shape(owned, 128),
            shape(2 * ghost, 3 * owned, dtype=bf16),
            put,
            put,
            cross,
            cross,
            shape(2 * ghost, 128),
        ),
        [m, up, dn],
        owned * owned,
    )
    ham_send = call(
        send_ham_kernel, shape(3 * ghost, 6 * ghost, dtype=bf16), [ham_halo, pick], 0
    )
    band = lax.axis_index("band")
    own_columns = lax.dynamic_slice_in_dim(rotation_store, band * cols, cols, 1)
    one = lax.ppermute(states, "band", flip(4, 1))
    two = lax.ppermute(states, "band", flip(4, 2))
    paired = doms == 8 and rotation_store.shape[0] % 16 == 0
    parts = [own_columns]
    if paired:
        parts += [lax.ppermute(own_columns, "dom", flip(doms, b)) for b in (2, 4, 6)]
    one, two, ham_own = lax.optimization_barrier((one, two, ham_own))
    longer = call(longer_kernel, shape(owned + 8, cols), [two], 0)
    three = lax.ppermute(longer, "band", flip(4, 1))
    two, *parts = lax.optimization_barrier((two, *parts))
    if paired:
        other = [lax.ppermute(part, "dom", near_pairs) for part in parts]
        slots = [part for pair in zip(parts, other) for part in pair]
        rotation = ordered_rotation(slots, owner, bands)
    else:
        columns = lax.all_gather(own_columns, "dom", axis=0, tiled=True)
        columns = columns.reshape(doms, -1, cols)[owner].reshape(bands, -1, cols)
        rotation = split(columns)
    work = 6 * owned * cols * cols
    total = call(rotate_kernel, block, [*rotation, states, one, two], 0)
    turned, to_near, to_far = call(
        rotate_last_kernel,
        (block, halo, halo),
        [*rotation, total, three, column, pick],
        work,
    )
    wide = shape(ext, cols)
    work = 6 * ext * ext * cols
    far, near = to_other(to_far), to_pair(to_near)
    partial, far_partial = call(
        first_partial_kernel, (wide, halo), [turned, column, ham_own, pick], work
    )
    to_near, sent, far_rows = call(
        first_sums_kernel,
        (halo, halo, halo),
        [far, near, partial, far_partial, to_far, ham_send, scales],
        0,
    )
    from_far, from_near = to_other(sent), to_pair(to_near)
    base = call(
        first_own_kernel, block, [far, near, partial, ham_halo, column, turned], 0
    )
    far = to_other(
        call(
            far_rows_kernel,
            shape(ghost, cols + 128),
            [from_near, far_rows, far_is_near, scales],
            0,
        )
    )
    base, near_rows = call(
        near_sums_kernel, (block, halo), [from_near, base, column, put_near, pick], 0
    )
    near = to_pair(
        call(near_rows_kernel, halo, [from_far, near_rows, near_is_far, scales], 0)
    )
    filtered = call(far_sums_kernel, block, [from_far, base, column, put_far], 0)
    partial = call(own_kernel, wide, [filtered, column, ham_own], work)
    to_near, to_far = call(
        second_sums_kernel, (halo, halo), [far, near, sent, partial, ham_halo], 0
    )
    from_far, from_near = to_other(to_far), to_pair(to_near)
    base = call(
        second_own_kernel,
        block,
        [far, near, sent, partial, ham_halo, column, filtered, turned],
        work,
    )
    operands = [from_far, base, from_near, column, put_near, put_far]
    return call(last_kernel, block, operands, small)


def solution(mesh):
    in_specs = (
        P("dom", "band"),
        P("dom"),
        P("dom", None, None),
        P("dom", None),
        P("dom"),
        P("dom"),
        P(),
        P("dom", None),
    )
    out_specs = P("dom", "band")
    return jax.shard_map(shards, mesh=mesh, in_specs=in_specs, out_specs=out_specs, check_vma=False)
```

```python
import functools

import jax
import jax.numpy as jnp
from jax import lax
from jax.experimental import pallas as pl
from jax.experimental.pallas import tpu as pltpu
from jax.sharding import PartitionSpec as P

filter_center = 2.5
filter_half = 3.5
spectrum_floor = -4.0
sigma_one = filter_half / (spectrum_floor - filter_center)
sigma_two = 1.0 / (2.0 / sigma_one - sigma_one)

f32 = jnp.float32
bf16 = jnp.bfloat16
VMEM_LIMIT = 32 * 1024 * 1024
VMEM_MOST = 56 * 1024 * 1024


def split(x):
    hi = x.astype(bf16)
    lo = (x - hi.astype(f32)).astype(bf16)
    return hi, lo


def mm(a, b, dims=((1,), (0,))):
    return lax.dot_general(a, b, (dims, ((), ())), preferred_element_type=f32)


def select(onehot, x):
    hi, lo = split(x)
    rest = (x - hi.astype(f32) - lo.astype(f32)).astype(bf16)
    return mm(onehot, hi) + mm(onehot, lo) + mm(onehot, rest)


def as_column(row):
    n = row.shape[1]
    here = lax.broadcasted_iota(jnp.int32, (n, n), 0) == lax.broadcasted_iota(jnp.int32, (n, n), 1)
    return jnp.sum(jnp.where(here, row, jnp.zeros_like(row)), axis=1, keepdims=True)


def pick_rows(list_row, owned):
    column = as_column(list_row.astype(f32)).astype(jnp.int32)
    shape = (list_row.shape[1], owned)
    return (lax.broadcasted_iota(jnp.int32, shape, 1) == column).astype(f32).astype(bf16)


def put_rows(list_row, owned):
    shape = (owned, list_row.shape[1])
    return (lax.broadcasted_iota(jnp.int32, shape, 0) == list_row).astype(f32).astype(bf16)


def call(kernel, out_shape, args, cost, **kwargs):
    vmem = pl.BlockSpec(memory_space=pltpu.VMEM)
    return pl.pallas_call(
        kernel,
        out_shape=out_shape,
        in_specs=[vmem] * len(args),
        out_specs=jax.tree.map(lambda _: vmem, out_shape),
        compiler_params=pltpu.CompilerParams(vmem_limit_bytes=VMEM_LIMIT),
        cost_estimate=pl.CostEstimate(flops=cost, bytes_accessed=min(cost, 1 << 20), transcendentals=0),
        **kwargs,
    )(*args)


def shape(*dims, dtype=f32):
    return jax.ShapeDtypeStruct(dims, dtype)


def lists_kernel(m, up, dn, column, pick, put_near, put_far, far_is_near, near_is_far, scales):
    owned = m.shape[1]
    column[...] = jnp.broadcast_to(as_column(m[...]), column.shape)
    even = lax.rem(lax.axis_index("dom"), 2) == 0
    up, dn = up[...], dn[...]
    near, far = jnp.where(even, up, dn), jnp.where(even, dn, up)
    rows = jnp.concatenate([pick_rows(near, owned), pick_rows(far, owned)], axis=0)
    pick[...] = jnp.concatenate([rows.astype(f32)] * 3, axis=1).astype(bf16)
    put_near[...] = jnp.concatenate([put_rows(near, owned).astype(f32)] * 3, axis=1).astype(bf16)
    put_far[...] = jnp.concatenate([put_rows(far, owned).astype(f32)] * 3, axis=1).astype(bf16)
    for out, these, those in ((far_is_near, far, near), (near_is_far, near, far)):
        same = as_column(these.astype(f32)) == those.astype(f32)
        out[...] = jnp.concatenate([same.astype(f32)] * 3, axis=1).astype(bf16)
    scales[...] = picked(column[...], pick[...])


def split_three(x):
    hi, lo = split(x)
    return hi, lo, (x - hi.astype(f32) - lo.astype(f32)).astype(bf16)


def picked(x, pick):
    return mm(pick, jnp.concatenate(split_three(x), axis=0))


def send_rows(x, pick, near_out, far_out):
    rows = picked(x, pick[...])
    ghost = near_out.shape[0]
    near_out[...] = rows[:ghost]
    far_out[...] = rows[ghost:]


def placed(rows, put):
    return mm(put[...], jnp.concatenate(split_three(rows[...]), axis=0))


def cell_term(ham, row, ext):
    n = ham.shape[0]
    gap = -n % 16
    hi, lo = split(jnp.concatenate([ham, jnp.zeros((gap, n), f32)], axis=0))
    spread = lax.broadcasted_iota(jnp.int32, (ext, n), 0) == row
    spread = spread.astype(f32)
    twice = jnp.concatenate([spread, jnp.zeros((ext, gap), f32), spread, jnp.zeros((ext, gap), f32)], axis=1)
    spread = spread.astype(bf16)
    left_hi, left_lo = split(mm(twice.astype(bf16), jnp.concatenate([hi, lo], axis=0)))
    wide = ext // 256 * 256
    both = mm(jnp.concatenate([left_hi, left_lo], axis=0), spread[:wide], ((1,), (1,)))
    rest = mm(
        jnp.concatenate([left_hi[wide:], left_lo[wide:]], axis=0), spread[wide:], ((1,), (1,))
    )
    return both[:ext] + both[ext:], rest[: ext - wide] + rest[ext - wide :]


def assemble_kernel(ghost, nodes_any, ham_any, own, halo, raw, ham, left, corner, sem):
    cells = ham.shape[0]
    ext, wide = left.shape
    owned = ext - 2 * ghost
    moves = [(nodes_any, raw)] + [(ham_any.at[c], ham.at[c]) for c in range(cells)]
    copies = [pltpu.make_async_copy(a, b, sem.at[i]) for i, (a, b) in enumerate(moves)]
    for copy in copies:
        copy.start()
    copies[0].wait()
    node = raw[...]
    lower = (node >= owned) & (node < owned + ghost)
    swapped = jnp.where(lower, node + ghost, jnp.where(node >= owned + ghost, node - ghost, node))
    nodes = jnp.where(lax.rem(lax.axis_index("dom"), 2) == 0, swapped, node)
    for c in range(cells):
        copies[1 + c].wait()
        term, rest = cell_term(ham[c], nodes[c : c + 1, :], ext)
        left[...] = term if c == 0 else left[...] + term
        corner[...] = rest if c == 0 else corner[...] + rest
    below = jnp.transpose(left[ext - 128 :, :])[:, 128 - (ext - wide) :]
    right = jnp.concatenate([below, corner[...]], axis=0)
    full = jnp.concatenate([left[...], right], axis=1)
    hi = full.astype(bf16).astype(f32)
    lo = full - hi
    for out, start, stop in ((own, 0, owned), (halo, owned, ext)):
        high = hi[:, start:stop]
        out[...] = jnp.concatenate([high, lo[:, start:stop], high], axis=1).astype(bf16)


def assemble(cell_nodes, cell_ham, ext, ghost):
    cells, n, _ = cell_ham.shape
    wide = ext // 256 * 256
    return pl.pallas_call(
        functools.partial(assemble_kernel, ghost),
        out_shape=(
            shape(ext, 3 * (ext - 2 * ghost), dtype=bf16),
            shape(ext, 6 * ghost, dtype=bf16),
        ),
        in_specs=[pl.BlockSpec(memory_space=pl.ANY)] * 2,
        out_specs=(pl.BlockSpec(memory_space=pltpu.VMEM),) * 2,
        scratch_shapes=[
            pltpu.VMEM((cells, n), jnp.int32),
            pltpu.VMEM((cells, n, n), f32),
            pltpu.VMEM((ext, wide), f32),
            pltpu.VMEM((ext - wide, ext - wide), f32),
            pltpu.SemaphoreType.DMA((1 + cells,)),
        ],
        compiler_params=pltpu.CompilerParams(vmem_limit_bytes=VMEM_MOST),
        cost_estimate=pl.CostEstimate(
            flops=cells * 8 * n * n * ext, bytes_accessed=cells * n * n * 4, transcendentals=0
        ),
    )(cell_nodes, cell_ham)


def own_kernel(v, column, ham, out):
    hi, lo = split(v[...] * column[:, :1])
    out[...] = mm(ham[...], jnp.concatenate([hi, hi, lo], axis=0))


def halo_part(near, far, ham):
    hi, lo = split(jnp.concatenate([near, far], axis=0))
    return mm(ham, jnp.concatenate([hi, hi, lo], axis=0))


def completed(far, sent):
    cols = sent.shape[1]
    scale = far[:, cols : cols + 1]
    return far[:, :cols] + (sigma_one / filter_half) * scale * scale * sent[...]


def send_ham_kernel(ham, pick, out):
    halo, owned = out.shape[0] * 2 // 3, pick.shape[1] // 3
    ghost = halo // 2
    out[:halo, :] = ham[owned:, :]
    out[halo:, :] = mm(pick[ghost:, :owned], ham[:owned, :]).astype(bf16)


def first_partial_kernel(v, column, ham, pick, out, far_out):
    own_kernel(v, column, ham, out)
    ghost = far_out.shape[0]
    far_out[...] = picked(out[: v.shape[0], :], pick[ghost:, :])


def first_sums_kernel(
    far, near, partial, far_partial, far_sent, ham, scales, to_near, to_far, far_rows
):
    ghost = near.shape[0]
    owned = partial.shape[0] - 2 * ghost
    z = halo_part(near[...], far[...], ham[...])
    to_near[...] = partial[owned : owned + ghost, :] + z[:ghost]
    to_far[...] = partial[owned + ghost :, :] + z[ghost : 2 * ghost]
    scale = scales[ghost:, :1]
    rows = scale * scale * (far_partial[...] + z[2 * ghost :])
    far_rows[...] = (sigma_one / filter_half) * (rows - filter_center * far_sent[...])


def first_own_kernel(far, near, partial, ham, column, s, base):
    owned = s.shape[0]
    z = partial[:owned, :] + halo_part(near[...], far[...], ham[:owned, :])
    base[...] = (sigma_one / filter_half) * (z * column[:, :1] - filter_center * s[...])


def far_rows_kernel(from_near, far_rows, far_is_near, scales, out):
    ghost, cols = far_rows.shape
    scale = scales[ghost:, :]
    added = (sigma_one / filter_half) * scale[:, :1] * scale[:, :1] * placed(from_near, far_is_near)
    out[...] = jnp.concatenate([far_rows[...] + added, scale], axis=1)


def near_sums_kernel(from_near, base, column, put_near, pick, out, near_rows):
    scale = column[:, :1]
    rows = base[...] + (sigma_one / filter_half) * scale * placed(from_near, put_near)
    out[...] = rows
    near_rows[...] = picked(rows * scale, pick[: near_rows.shape[0], :])


def near_rows_kernel(from_far, near_rows, near_is_far, scales, out):
    scale = scales[: out.shape[0], :1]
    added = (sigma_one / filter_half) * scale * scale * placed(from_far, near_is_far)
    out[...] = near_rows[...] + added


def far_sums_kernel(from_far, base, column, put_far, one):
    scale = (sigma_one / filter_half) * column[:, :1]
    one[...] = base[...] + scale * placed(from_far, put_far)


def second_sums_kernel(far, near, sent, partial, ham, to_near, to_far):
    ghost = near.shape[0]
    owned = partial.shape[0] - 2 * ghost
    z = partial[owned:, :] + halo_part(near[...], completed(far, sent), ham[owned:, :])
    to_near[...] = z[:ghost]
    to_far[...] = z[ghost:]


def second_own_kernel(far, near, sent, partial, ham, column, one, s, base):
    owned = s.shape[0]
    z = partial[:owned, :] + halo_part(near[...], completed(far, sent), ham[:owned, :])
    base[...] = (
        2.0 * sigma_two / filter_half * (z * column[:, :1] - filter_center * one[...])
        - sigma_one * sigma_two * s[...]
    )


def last_kernel(from_far, base, from_near, column, put_near, put_far, out):
    sums = placed(from_near, put_near) + placed(from_far, put_far)
    out[...] = base[...] + 2.0 * sigma_two / filter_half * column[:, :1] * sums


def order_kernel(owner, *refs):
    parts, (hi_out, lo_out) = refs[:-2], refs[-2:]
    here = lax.axis_index("dom")
    panel = lax.broadcasted_iota(jnp.int32, owner.shape, 1).astype(f32)
    for b, part in enumerate(parts):
        place = jnp.sum(jnp.where(owner[...] == (here ^ b), panel, 0.0)).astype(jnp.int32)
        hi, lo = split(part[...])
        hi_out[place] = hi
        lo_out[place] = lo


def left_side(rows):
    hi, lo = split(rows)
    return jnp.concatenate([hi, lo, hi], axis=1)


def rotated(left, hi_ref, lo_ref, distance):
    k = lax.axis_index("band") ^ distance
    rhi, rlo = hi_ref[k], lo_ref[k]
    return mm(left, jnp.concatenate([rhi, rhi, rlo], axis=0))


def left_kernel(own, one, two, out):
    for r, block in enumerate((own, one, two)):
        out[r] = left_side(block[...])


def longer_kernel(block, out):
    rows = block.shape[0]
    out[:rows, :] = block[...]
    out[rows:, :] = block[: out.shape[0] - rows, :]


def rotate_kernel(hi_ref, lo_ref, left, out):
    out[...] = sum(rotated(left[r], hi_ref, lo_ref, r) for r in range(left.shape[0]))


def rotate_last_kernel(hi_ref, lo_ref, total, three, column, pick, out, near_out, far_out):
    left = left_side(three[: total.shape[0], :])
    rows = total[...] + rotated(left, hi_ref, lo_ref, 3)
    out[...] = rows
    send_rows(rows * column[:, :1], pick, near_out, far_out)


def flip(count, bits):
    return [(i, i ^ bits) for i in range(count)]


def ordered_rotation(slots, owner, bands):
    rows, cols = slots[0].shape
    total = len(slots) * rows
    hi, lo = call(
        order_kernel,
        (shape(len(slots), rows, cols, dtype=bf16),) * 2,
        [owner[None, :], *slots],
        0,
    )
    return hi.reshape(bands, total // bands, cols), lo.reshape(bands, total // bands, cols)


def shards(states, inv_mass, cell_ham, cell_nodes, send_up, send_down, owner, rotation_store):
    owned, cols = states.shape
    ghost = send_up.shape[0]
    ext = owned + 2 * ghost
    doms, bands = lax.axis_size("dom"), lax.axis_size("band")
    m = inv_mass[None, :]
    up = send_up[None, :]
    dn = send_down[None, :]
    near_pairs = flip(doms, 1)
    far_pairs = [(i, (i - 1 if i % 2 == 0 else i + 1) % doms) for i in range(doms)]
    halo = shape(ghost, cols)
    block = shape(owned, cols)
    small = 4 * ghost * owned * cols * 3

    def to_pair(rows):
        return lax.ppermute(rows, "dom", near_pairs)

    def to_other(rows):
        return lax.ppermute(rows, "dom", far_pairs)

    ham_own, ham_halo = assemble(cell_nodes, cell_ham, ext, ghost)
    put = shape(owned, 3 * ghost, dtype=bf16)
    cross = shape(ghost, 3 * ghost, dtype=bf16)
    column, pick, put_near, put_far, far_is_near, near_is_far, scales = call(
        lists_kernel,
        (
            shape(owned, 128),
            shape(2 * ghost, 3 * owned, dtype=bf16),
            put,
            put,
            cross,
            cross,
            shape(2 * ghost, 128),
        ),
        [m, up, dn],
        owned * owned,
    )
    ham_send = call(
        send_ham_kernel, shape(3 * ghost, 6 * ghost, dtype=bf16), [ham_halo, pick], 0
    )
    band = lax.axis_index("band")
    own_columns = lax.dynamic_slice_in_dim(rotation_store, band * cols, cols, 1)
    one = lax.ppermute(states, "band", flip(4, 1))
    two = lax.ppermute(states, "band", flip(4, 2))
    paired = doms == 8 and rotation_store.shape[0] % 16 == 0
    parts = [own_columns]
    if paired:
        parts += [lax.ppermute(own_columns, "dom", flip(doms, b)) for b in (2, 4, 6)]
    one, two, ham_own = lax.optimization_barrier((one, two, ham_own))
    longer = call(longer_kernel, shape(owned + 8, cols), [two], 0)
    three = lax.ppermute(longer, "band", flip(4, 1))
    left = call(left_kernel, shape(3, owned, 3 * cols, dtype=bf16), [states, one, two], 0)
    left, *parts = lax.optimization_barrier((left, *parts))
    if paired:
        other = [lax.ppermute(part, "dom", near_pairs) for part in parts]
        slots = [part for pair in zip(parts, other) for part in pair]
        rotation = ordered_rotation(slots, owner, bands)
    else:
        columns = lax.all_gather(own_columns, "dom", axis=0, tiled=True)
        columns = columns.reshape(doms, -1, cols)[owner].reshape(bands, -1, cols)
        rotation = split(columns)
    work = 6 * owned * cols * cols
    total = call(rotate_kernel, block, [*rotation, left], 0)
    turned, to_near, to_far = call(
        rotate_last_kernel,
        (block, halo, halo),
        [*rotation, total, three, column, pick],
        work,
    )
    wide = shape(ext, cols)
    work = 6 * ext * ext * cols
    far, near = to_other(to_far), to_pair(to_near)
    partial, far_partial = call(
        first_partial_kernel, (wide, halo), [turned, column, ham_own, pick], work
    )
    to_near, sent, far_rows = call(
        first_sums_kernel,
        (halo, halo, halo),
        [far, near, partial, far_partial, to_far, ham_send, scales],
        0,
    )
    from_far, from_near = to_other(sent), to_pair(to_near)
    base = call(
        first_own_kernel, block, [far, near, partial, ham_halo, column, turned], 0
    )
    far = to_other(
        call(
            far_rows_kernel,
            shape(ghost, cols + 128),
            [from_near, far_rows, far_is_near, scales],
            0,
        )
    )
    base, near_rows = call(
        near_sums_kernel, (block, halo), [from_near, base, column, put_near, pick], 0
    )
    near = to_pair(
        call(near_rows_kernel, halo, [from_far, near_rows, near_is_far, scales], 0)
    )
    filtered = call(far_sums_kernel, block, [from_far, base, column, put_far], 0)
    partial = call(own_kernel, wide, [filtered, column, ham_own], work)
    to_near, to_far = call(
        second_sums_kernel, (halo, halo), [far, near, sent, partial, ham_halo], 0
    )
    from_far, from_near = to_other(to_far), to_pair(to_near)
    base = call(
        second_own_kernel,
        block,
        [far, near, sent, partial, ham_halo, column, filtered, turned],
        work,
    )
    operands = [from_far, base, from_near, column, put_near, put_far]
    return call(last_kernel, block, operands, small)


def solution(mesh):
    in_specs = (
        P("dom", "band"),
        P("dom"),
        P("dom", None, None),
        P("dom", None),
        P("dom"),
        P("dom"),
        P(),
        P("dom", None),
    )
    out_specs = P("dom", "band")
    return jax.shard_map(shards, mesh=mesh, in_specs=in_specs, out_specs=out_specs, check_vma=False)
```

```python
import functools

import jax
import jax.numpy as jnp
from jax import lax
from jax.experimental import pallas as pl
from jax.experimental.pallas import tpu as pltpu
from jax.sharding import PartitionSpec as P

filter_center = 2.5
filter_half = 3.5
spectrum_floor = -4.0
sigma_one = filter_half / (spectrum_floor - filter_center)
sigma_two = 1.0 / (2.0 / sigma_one - sigma_one)

f32 = jnp.float32
bf16 = jnp.bfloat16
VMEM_LIMIT = 32 * 1024 * 1024
VMEM_MOST = 56 * 1024 * 1024


def split(x):
    hi = x.astype(bf16)
    lo = (x - hi.astype(f32)).astype(bf16)
    return hi, lo


def mm(a, b, dims=((1,), (0,))):
    return lax.dot_general(a, b, (dims, ((), ())), preferred_element_type=f32)


def as_column(row):
    n = row.shape[1]
    here = lax.broadcasted_iota(jnp.int32, (n, n), 0) == lax.broadcasted_iota(jnp.int32, (n, n), 1)
    return jnp.sum(jnp.where(here, row, jnp.zeros_like(row)), axis=1, keepdims=True)


def pick_rows(list_row, owned):
    column = as_column(list_row.astype(f32)).astype(jnp.int32)
    shape = (list_row.shape[1], owned)
    return (lax.broadcasted_iota(jnp.int32, shape, 1) == column).astype(f32).astype(bf16)


def put_rows(list_row, owned):
    shape = (owned, list_row.shape[1])
    return (lax.broadcasted_iota(jnp.int32, shape, 0) == list_row).astype(f32).astype(bf16)


def call(kernel, out_shape, args, cost, **kwargs):
    vmem = pl.BlockSpec(memory_space=pltpu.VMEM)
    return pl.pallas_call(
        kernel,
        out_shape=out_shape,
        in_specs=[vmem] * len(args),
        out_specs=jax.tree.map(lambda _: vmem, out_shape),
        compiler_params=pltpu.CompilerParams(vmem_limit_bytes=VMEM_LIMIT),
        cost_estimate=pl.CostEstimate(flops=cost, bytes_accessed=min(cost, 1 << 20), transcendentals=0),
        **kwargs,
    )(*args)


def shape(*dims, dtype=f32):
    return jax.ShapeDtypeStruct(dims, dtype)


def lists_kernel(m, up, dn, column, pick, put_near, put_far, far_is_near, near_is_far, scales):
    owned = m.shape[1]
    column[...] = jnp.broadcast_to(as_column(m[...]), column.shape)
    even = lax.rem(lax.axis_index("dom"), 2) == 0
    up, dn = up[...], dn[...]
    near, far = jnp.where(even, up, dn), jnp.where(even, dn, up)
    rows = jnp.concatenate([pick_rows(near, owned), pick_rows(far, owned)], axis=0)
    pick[...] = jnp.concatenate([rows.astype(f32)] * 2, axis=1).astype(bf16)
    put_near[...] = jnp.concatenate([put_rows(near, owned).astype(f32)] * 2, axis=1).astype(bf16)
    put_far[...] = jnp.concatenate([put_rows(far, owned).astype(f32)] * 2, axis=1).astype(bf16)
    for out, these, those in ((far_is_near, far, near), (near_is_far, near, far)):
        same = as_column(these.astype(f32)) == those.astype(f32)
        out[...] = jnp.concatenate([same.astype(f32)] * 2, axis=1).astype(bf16)
    scales[...] = picked(column[...], pick[...])


def picked(x, pick):
    return mm(pick, jnp.concatenate(split(x), axis=0))


def send_rows(x, pick, near_out, far_out):
    rows = picked(x, pick[...])
    ghost = near_out.shape[0]
    near_out[...] = rows[:ghost]
    far_out[...] = rows[ghost:]


def placed(rows, put):
    return mm(put[...], jnp.concatenate(split(rows[...]), axis=0))


def cell_term(ham, row, ext):
    n = ham.shape[0]
    gap = -n % 16
    hi, lo = split(jnp.concatenate([ham, jnp.zeros((gap, n), f32)], axis=0))
    spread = lax.broadcasted_iota(jnp.int32, (ext, n), 0) == row
    spread = spread.astype(f32)
    twice = jnp.concatenate([spread, jnp.zeros((ext, gap), f32), spread, jnp.zeros((ext, gap), f32)], axis=1)
    spread = spread.astype(bf16)
    left_hi, left_lo = split(mm(twice.astype(bf16), jnp.concatenate([hi, lo], axis=0)))
    wide = ext // 256 * 256
    both = mm(jnp.concatenate([left_hi, left_lo], axis=0), spread[:wide], ((1,), (1,)))
    rest = mm(
        jnp.concatenate([left_hi[wide:], left_lo[wide:]], axis=0), spread[wide:], ((1,), (1,))
    )
    return both[:ext] + both[ext:], rest[: ext - wide] + rest[ext - wide :]


def assemble_kernel(ghost, nodes_any, ham_any, own, halo, raw, ham, left, corner, sem):
    cells = ham.shape[0]
    ext, wide = left.shape
    owned = ext - 2 * ghost
    moves = [(nodes_any, raw)] + [(ham_any.at[c], ham.at[c]) for c in range(cells)]
    copies = [pltpu.make_async_copy(a, b, sem.at[i]) for i, (a, b) in enumerate(moves)]
    for copy in copies:
        copy.start()
    copies[0].wait()
    node = raw[...]
    lower = (node >= owned) & (node < owned + ghost)
    swapped = jnp.where(lower, node + ghost, jnp.where(node >= owned + ghost, node - ghost, node))
    nodes = jnp.where(lax.rem(lax.axis_index("dom"), 2) == 0, swapped, node)
    for c in range(cells):
        copies[1 + c].wait()
        term, rest = cell_term(ham[c], nodes[c : c + 1, :], ext)
        left[...] = term if c == 0 else left[...] + term
        corner[...] = rest if c == 0 else corner[...] + rest
    below = jnp.transpose(left[ext - 128 :, :])[:, 128 - (ext - wide) :]
    right = jnp.concatenate([below, corner[...]], axis=0)
    full = jnp.concatenate([left[...], right], axis=1)
    hi = full.astype(bf16).astype(f32)
    lo = full - hi
    for out, start, stop in ((own, 0, owned), (halo, owned, ext)):
        high = hi[:, start:stop]
        out[...] = jnp.concatenate([high, lo[:, start:stop], high], axis=1).astype(bf16)


def assemble(cell_nodes, cell_ham, ext, ghost):
    cells, n, _ = cell_ham.shape
    wide = ext // 256 * 256
    return pl.pallas_call(
        functools.partial(assemble_kernel, ghost),
        out_shape=(
            shape(ext, 3 * (ext - 2 * ghost), dtype=bf16),
            shape(ext, 6 * ghost, dtype=bf16),
        ),
        in_specs=[pl.BlockSpec(memory_space=pl.ANY)] * 2,
        out_specs=(pl.BlockSpec(memory_space=pltpu.VMEM),) * 2,
        scratch_shapes=[
            pltpu.VMEM((cells, n), jnp.int32),
            pltpu.VMEM((cells, n, n), f32),
            pltpu.VMEM((ext, wide), f32),
            pltpu.VMEM((ext - wide, ext - wide), f32),
            pltpu.SemaphoreType.DMA((1 + cells,)),
        ],
        compiler_params=pltpu.CompilerParams(vmem_limit_bytes=VMEM_MOST),
        cost_estimate=pl.CostEstimate(
            flops=cells * 8 * n * n * ext, bytes_accessed=cells * n * n * 4, transcendentals=0
        ),
    )(cell_nodes, cell_ham)


def own_kernel(v, column, ham, out):
    hi, lo = split(v[...] * column[:, :1])
    out[...] = mm(ham[...], jnp.concatenate([hi, hi, lo], axis=0))


def halo_part(near, far, ham):
    hi, lo = split(jnp.concatenate([near, far], axis=0))
    return mm(ham, jnp.concatenate([hi, hi, lo], axis=0))


def completed(far, sent):
    cols = sent.shape[1]
    scale = far[:, cols : cols + 1]
    return far[:, :cols] + (sigma_one / filter_half) * scale * scale * sent[...]


def send_ham_kernel(ham, pick, out):
    halo, owned = out.shape[0] * 2 // 3, pick.shape[1] // 2
    ghost = halo // 2
    out[:halo, :] = ham[owned:, :]
    out[halo:, :] = mm(pick[ghost:, :owned], ham[:owned, :]).astype(bf16)


def first_partial_kernel(v, column, ham, pick, out, far_out):
    own_kernel(v, column, ham, out)
    ghost = far_out.shape[0]
    far_out[...] = picked(out[: v.shape[0], :], pick[ghost:, :])


def first_sums_kernel(
    far, near, partial, far_partial, far_sent, ham, scales, to_near, to_far, far_rows
):
    ghost = near.shape[0]
    owned = partial.shape[0] - 2 * ghost
    z = halo_part(near[...], far[...], ham[...])
    to_near[...] = partial[owned : owned + ghost, :] + z[:ghost]
    to_far[...] = partial[owned + ghost :, :] + z[ghost : 2 * ghost]
    scale = scales[ghost:, :1]
    rows = scale * scale * (far_partial[...] + z[2 * ghost :])
    far_rows[...] = (sigma_one / filter_half) * (rows - filter_center * far_sent[...])


def first_own_kernel(far, near, partial, ham, column, s, base):
    owned = s.shape[0]
    z = partial[:owned, :] + halo_part(near[...], far[...], ham[:owned, :])
    base[...] = (sigma_one / filter_half) * (z * column[:, :1] - filter_center * s[...])


def far_rows_kernel(from_near, far_rows, far_is_near, scales, out):
    ghost, cols = far_rows.shape
    scale = scales[ghost:, :]
    added = (sigma_one / filter_half) * scale[:, :1] * scale[:, :1] * placed(from_near, far_is_near)
    out[...] = jnp.concatenate([far_rows[...] + added, scale], axis=1)


def near_sums_kernel(from_near, base, column, put_near, pick, out, near_rows):
    scale = column[:, :1]
    rows = base[...] + (sigma_one / filter_half) * scale * placed(from_near, put_near)
    out[...] = rows
    near_rows[...] = picked(rows * scale, pick[: near_rows.shape[0], :])


def near_rows_kernel(from_far, near_rows, near_is_far, scales, out):
    scale = scales[: out.shape[0], :1]
    added = (sigma_one / filter_half) * scale * scale * placed(from_far, near_is_far)
    out[...] = near_rows[...] + added


def far_sums_kernel(from_far, base, column, put_far, one):
    scale = (sigma_one / filter_half) * column[:, :1]
    one[...] = base[...] + scale * placed(from_far, put_far)


def second_sums_kernel(far, near, sent, partial, ham, to_near, to_far):
    ghost = near.shape[0]
    owned = partial.shape[0] - 2 * ghost
    z = partial[owned:, :] + halo_part(near[...], completed(far, sent), ham[owned:, :])
    to_near[...] = z[:ghost]
    to_far[...] = z[ghost:]


def second_own_kernel(far, near, sent, partial, ham, column, one, s, base):
    owned = s.shape[0]
    z = partial[:owned, :] + halo_part(near[...], completed(far, sent), ham[:owned, :])
    base[...] = (
        2.0 * sigma_two / filter_half * (z * column[:, :1] - filter_center * one[...])
        - sigma_one * sigma_two * s[...]
    )


def last_kernel(from_far, base, from_near, column, put_near, put_far, out):
    sums = placed(from_near, put_near) + placed(from_far, put_far)
    out[...] = base[...] + 2.0 * sigma_two / filter_half * column[:, :1] * sums


def order_kernel(owner, *refs):
    parts, (hi_out, lo_out) = refs[:-2], refs[-2:]
    here = lax.axis_index("dom")
    panel = lax.broadcasted_iota(jnp.int32, owner.shape, 1).astype(f32)
    for b, part in enumerate(parts):
        place = jnp.sum(jnp.where(owner[...] == (here ^ b), panel, 0.0)).astype(jnp.int32)
        hi, lo = split(part[...])
        hi_out[place] = hi
        lo_out[place] = lo


def left_side(rows):
    hi, lo = split(rows)
    return jnp.concatenate([hi, lo, hi], axis=1)


def rotated(left, hi_ref, lo_ref, distance):
    k = lax.axis_index("band") ^ distance
    rhi, rlo = hi_ref[k], lo_ref[k]
    return mm(left, jnp.concatenate([rhi, rhi, rlo], axis=0))


def left_kernel(own, one, two, out):
    for r, block in enumerate((own, one, two)):
        out[r] = left_side(block[...])


def longer_kernel(block, out):
    rows = block.shape[0]
    out[:rows, :] = block[...]
    out[rows:, :] = block[: out.shape[0] - rows, :]


def rotate_kernel(hi_ref, lo_ref, left, out):
    out[...] = sum(rotated(left[r], hi_ref, lo_ref, r) for r in range(left.shape[0]))


def rotate_last_kernel(hi_ref, lo_ref, total, three, column, pick, out, near_out, far_out):
    left = left_side(three[: total.shape[0], :])
    rows = total[...] + rotated(left, hi_ref, lo_ref, 3)
    out[...] = rows
    send_rows(rows * column[:, :1], pick, near_out, far_out)


def flip(count, bits):
    return [(i, i ^ bits) for i in range(count)]


def ordered_rotation(slots, owner, bands):
    rows, cols = slots[0].shape
    total = len(slots) * rows
    hi, lo = call(
        order_kernel,
        (shape(len(slots), rows, cols, dtype=bf16),) * 2,
        [owner[None, :], *slots],
        0,
    )
    return hi.reshape(bands, total // bands, cols), lo.reshape(bands, total // bands, cols)


def shards(states, inv_mass, cell_ham, cell_nodes, send_up, send_down, owner, rotation_store):
    owned, cols = states.shape
    ghost = send_up.shape[0]
    ext = owned + 2 * ghost
    doms, bands = lax.axis_size("dom"), lax.axis_size("band")
    m = inv_mass[None, :]
    up = send_up[None, :]
    dn = send_down[None, :]
    near_pairs = flip(doms, 1)
    far_pairs = [(i, (i - 1 if i % 2 == 0 else i + 1) % doms) for i in range(doms)]
    halo = shape(ghost, cols)
    block = shape(owned, cols)
    small = 4 * ghost * owned * cols * 3

    def to_pair(rows):
        return lax.ppermute(rows, "dom", near_pairs)

    def to_other(rows):
        return lax.ppermute(rows, "dom", far_pairs)

    ham_own, ham_halo = assemble(cell_nodes, cell_ham, ext, ghost)
    put = shape(owned, 2 * ghost, dtype=bf16)
    cross = shape(ghost, 2 * ghost, dtype=bf16)
    column, pick, put_near, put_far, far_is_near, near_is_far, scales = call(
        lists_kernel,
        (
            shape(owned, 128),
            shape(2 * ghost, 2 * owned, dtype=bf16),
            put,
            put,
            cross,
            cross,
            shape(2 * ghost, 128),
        ),
        [m, up, dn],
        owned * owned,
    )
    ham_send = call(
        send_ham_kernel, shape(3 * ghost, 6 * ghost, dtype=bf16), [ham_halo, pick], 0
    )
    band = lax.axis_index("band")
    own_columns = lax.dynamic_slice_in_dim(rotation_store, band * cols, cols, 1)
    one = lax.ppermute(states, "band", flip(4, 1))
    two = lax.ppermute(states, "band", flip(4, 2))
    paired = doms == 8 and rotation_store.shape[0] % 16 == 0
    parts = [own_columns]
    if paired:
        parts += [lax.ppermute(own_columns, "dom", flip(doms, b)) for b in (2, 4, 6)]
    one, two, ham_own = lax.optimization_barrier((one, two, ham_own))
    longer = call(longer_kernel, shape(owned + 8, cols), [two], 0)
    three = lax.ppermute(longer, "band", flip(4, 1))
    left = call(left_kernel, shape(3, owned, 3 * cols, dtype=bf16), [states, one, two], 0)
    left, *parts = lax.optimization_barrier((left, *parts))
    if paired:
        other = [lax.ppermute(part, "dom", near_pairs) for part in parts]
        slots = [part for pair in zip(parts, other) for part in pair]
        rotation = ordered_rotation(slots, owner, bands)
    else:
        columns = lax.all_gather(own_columns, "dom", axis=0, tiled=True)
        columns = columns.reshape(doms, -1, cols)[owner].reshape(bands, -1, cols)
        rotation = split(columns)
    work = 6 * owned * cols * cols
    total = call(rotate_kernel, block, [*rotation, left], 0)
    turned, to_near, to_far = call(
        rotate_last_kernel,
        (block, halo, halo),
        [*rotation, total, three, column, pick],
        work,
    )
    wide = shape(ext, cols)
    work = 6 * ext * ext * cols
    far, near = to_other(to_far), to_pair(to_near)
    partial, far_partial = call(
        first_partial_kernel, (wide, halo), [turned, column, ham_own, pick], work
    )
    to_near, sent, far_rows = call(
        first_sums_kernel,
        (halo, halo, halo),
        [far, near, partial, far_partial, to_far, ham_send, scales],
        0,
    )
    from_far, from_near = to_other(sent), to_pair(to_near)
    base = call(
        first_own_kernel, block, [far, near, partial, ham_halo, column, turned], 0
    )
    far = to_other(
        call(
            far_rows_kernel,
            shape(ghost, cols + 128),
            [from_near, far_rows, far_is_near, scales],
            0,
        )
    )
    base, near_rows = call(
        near_sums_kernel, (block, halo), [from_near, base, column, put_near, pick], 0
    )
    near = to_pair(
        call(near_rows_kernel, halo, [from_far, near_rows, near_is_far, scales], 0)
    )
    filtered = call(far_sums_kernel, block, [from_far, base, column, put_far], 0)
    partial = call(own_kernel, wide, [filtered, column, ham_own], work)
    to_near, to_far = call(
        second_sums_kernel, (halo, halo), [far, near, sent, partial, ham_halo], 0
    )
    from_far, from_near = to_other(to_far), to_pair(to_near)
    base = call(
        second_own_kernel,
        block,
        [far, near, sent, partial, ham_halo, column, filtered, turned],
        work,
    )
    operands = [from_far, base, from_near, column, put_near, put_far]
    return call(last_kernel, block, operands, small)


def solution(mesh):
    in_specs = (
        P("dom", "band"),
        P("dom"),
        P("dom", None, None),
        P("dom", None),
        P("dom"),
        P("dom"),
        P(),
        P("dom", None),
    )
    out_specs = P("dom", "band")
    return jax.shard_map(shards, mesh=mesh, in_specs=in_specs, out_specs=out_specs, check_vma=False)
```

```python
import functools

import jax
import jax.numpy as jnp
from jax import lax
from jax.experimental import pallas as pl
from jax.experimental.pallas import tpu as pltpu
from jax.sharding import PartitionSpec as P

filter_center = 2.5
filter_half = 3.5
spectrum_floor = -4.0
sigma_one = filter_half / (spectrum_floor - filter_center)
sigma_two = 1.0 / (2.0 / sigma_one - sigma_one)

f32 = jnp.float32
bf16 = jnp.bfloat16
VMEM_LIMIT = 32 * 1024 * 1024
VMEM_MOST = 56 * 1024 * 1024


def split(x):
    hi = x.astype(bf16)
    lo = (x - hi.astype(f32)).astype(bf16)
    return hi, lo


def mm(a, b, dims=((1,), (0,))):
    return lax.dot_general(a, b, (dims, ((), ())), preferred_element_type=f32)


def as_column(row):
    n = row.shape[1]
    here = lax.broadcasted_iota(jnp.int32, (n, n), 0) == lax.broadcasted_iota(jnp.int32, (n, n), 1)
    return jnp.sum(jnp.where(here, row, jnp.zeros_like(row)), axis=1, keepdims=True)


def pick_rows(list_row, owned):
    column = as_column(list_row.astype(f32)).astype(jnp.int32)
    shape = (list_row.shape[1], owned)
    return (lax.broadcasted_iota(jnp.int32, shape, 1) == column).astype(f32).astype(bf16)


def put_rows(list_row, owned):
    shape = (owned, list_row.shape[1])
    return (lax.broadcasted_iota(jnp.int32, shape, 0) == list_row).astype(f32).astype(bf16)


def call(kernel, out_shape, args, cost, **kwargs):
    vmem = pl.BlockSpec(memory_space=pltpu.VMEM)
    return pl.pallas_call(
        kernel,
        out_shape=out_shape,
        in_specs=[vmem] * len(args),
        out_specs=jax.tree.map(lambda _: vmem, out_shape),
        compiler_params=pltpu.CompilerParams(vmem_limit_bytes=VMEM_LIMIT),
        cost_estimate=pl.CostEstimate(flops=cost, bytes_accessed=min(cost, 1 << 20), transcendentals=0),
        **kwargs,
    )(*args)


def shape(*dims, dtype=f32):
    return jax.ShapeDtypeStruct(dims, dtype)


def lists_kernel(m, up, dn, column, pick, put_near, put_far, far_is_near, near_is_far, scales):
    owned = m.shape[1]
    column[...] = jnp.broadcast_to(as_column(m[...]), column.shape)
    even = lax.rem(lax.axis_index("dom"), 2) == 0
    up, dn = up[...], dn[...]
    near, far = jnp.where(even, up, dn), jnp.where(even, dn, up)
    rows = jnp.concatenate([pick_rows(near, owned), pick_rows(far, owned)], axis=0)
    pick[...] = jnp.concatenate([rows.astype(f32)] * 2, axis=1).astype(bf16)
    put_near[...] = jnp.concatenate([put_rows(near, owned).astype(f32)] * 2, axis=1).astype(bf16)
    put_far[...] = jnp.concatenate([put_rows(far, owned).astype(f32)] * 2, axis=1).astype(bf16)
    for out, these, those in ((far_is_near, far, near), (near_is_far, near, far)):
        same = as_column(these.astype(f32)) == those.astype(f32)
        out[...] = jnp.concatenate([same.astype(f32)] * 2, axis=1).astype(bf16)
    scales[...] = picked(column[...], pick[...])


def picked(x, pick):
    return mm(pick, jnp.concatenate(split(x), axis=0))


def send_rows(x, pick, near_out, far_out):
    rows = picked(x, pick[...])
    ghost = near_out.shape[0]
    near_out[...] = rows[:ghost]
    far_out[...] = rows[ghost:]


def placed(rows, put):
    return mm(put[...], jnp.concatenate(split(rows[...]), axis=0))


def cell_term(ham, row, ext):
    n = ham.shape[0]
    gap = -n % 16
    hi, lo = split(jnp.concatenate([ham, jnp.zeros((gap, n), f32)], axis=0))
    spread = lax.broadcasted_iota(jnp.int32, (ext, n), 0) == row
    spread = spread.astype(f32)
    twice = jnp.concatenate([spread, jnp.zeros((ext, gap), f32), spread, jnp.zeros((ext, gap), f32)], axis=1)
    spread = spread.astype(bf16)
    left_hi, left_lo = split(mm(twice.astype(bf16), jnp.concatenate([hi, lo], axis=0)))
    wide = ext // 256 * 256
    both = mm(jnp.concatenate([left_hi, left_lo], axis=0), spread[:wide], ((1,), (1,)))
    rest = mm(
        jnp.concatenate([left_hi[wide:], left_lo[wide:]], axis=0), spread[wide:], ((1,), (1,))
    )
    return both[:ext] + both[ext:], rest[: ext - wide] + rest[ext - wide :]


def assemble_kernel(ghost, nodes_any, ham_any, own, halo, raw, ham, left, corner, sem):
    cells = ham.shape[0]
    ext, wide = left.shape
    owned = ext - 2 * ghost
    moves = [(nodes_any, raw)] + [(ham_any.at[c], ham.at[c]) for c in range(cells)]
    copies = [pltpu.make_async_copy(a, b, sem.at[i]) for i, (a, b) in enumerate(moves)]
    for copy in copies:
        copy.start()
    copies[0].wait()
    node = raw[...]
    lower = (node >= owned) & (node < owned + ghost)
    swapped = jnp.where(lower, node + ghost, jnp.where(node >= owned + ghost, node - ghost, node))
    nodes = jnp.where(lax.rem(lax.axis_index("dom"), 2) == 0, swapped, node)
    for c in range(cells):
        copies[1 + c].wait()
        term, rest = cell_term(ham[c], nodes[c : c + 1, :], ext)
        left[...] = term if c == 0 else left[...] + term
        corner[...] = rest if c == 0 else corner[...] + rest
    below = jnp.transpose(left[ext - 128 :, :])[:, 128 - (ext - wide) :]
    right = jnp.concatenate([below, corner[...]], axis=0)
    full = jnp.concatenate([left[...], right], axis=1)
    hi = full.astype(bf16).astype(f32)
    lo = full - hi
    for out, start, stop in ((own, 0, owned), (halo, owned, ext)):
        high = hi[:, start:stop]
        out[...] = jnp.concatenate([high, lo[:, start:stop], high], axis=1).astype(bf16)


def assemble(cell_nodes, cell_ham, ext, ghost):
    cells, n, _ = cell_ham.shape
    wide = ext // 256 * 256
    return pl.pallas_call(
        functools.partial(assemble_kernel, ghost),
        out_shape=(
            shape(ext, 3 * (ext - 2 * ghost), dtype=bf16),
            shape(ext, 6 * ghost, dtype=bf16),
        ),
        in_specs=[pl.BlockSpec(memory_space=pl.ANY)] * 2,
        out_specs=(pl.BlockSpec(memory_space=pltpu.VMEM),) * 2,
        scratch_shapes=[
            pltpu.VMEM((cells, n), jnp.int32),
            pltpu.VMEM((cells, n, n), f32),
            pltpu.VMEM((ext, wide), f32),
            pltpu.VMEM((ext - wide, ext - wide), f32),
            pltpu.SemaphoreType.DMA((1 + cells,)),
        ],
        compiler_params=pltpu.CompilerParams(vmem_limit_bytes=VMEM_MOST),
        cost_estimate=pl.CostEstimate(
            flops=cells * 8 * n * n * ext, bytes_accessed=cells * n * n * 4, transcendentals=0
        ),
    )(cell_nodes, cell_ham)


def own_kernel(v, column, ham, out):
    hi, lo = split(v[...] * column[:, :1])
    out[...] = mm(ham[...], jnp.concatenate([hi, hi, lo], axis=0))


def halo_part(near, far, ham):
    hi, lo = split(jnp.concatenate([near, far], axis=0))
    return mm(ham, jnp.concatenate([hi, hi, lo], axis=0))


def completed(far, sent):
    cols = sent.shape[1]
    scale = far[:, cols : cols + 1]
    return far[:, :cols] + (sigma_one / filter_half) * scale * scale * sent[...]


def send_ham_kernel(ham, pick, out):
    halo, owned = out.shape[0] * 2 // 3, pick.shape[1] // 2
    ghost = halo // 2
    out[:halo, :] = ham[owned:, :]
    out[halo:, :] = mm(pick[ghost:, :owned], ham[:owned, :]).astype(bf16)


def first_partial_kernel(v, column, ham, pick, out, far_out):
    own_kernel(v, column, ham, out)
    ghost = far_out.shape[0]
    far_out[...] = picked(out[: v.shape[0], :], pick[ghost:, :])


def first_sums_kernel(
    far, near, partial, far_partial, far_sent, ham, scales, to_near, to_far, far_rows
):
    ghost = near.shape[0]
    owned = partial.shape[0] - 2 * ghost
    z = halo_part(near[...], far[...], ham[...])
    to_near[...] = partial[owned : owned + ghost, :] + z[:ghost]
    to_far[...] = partial[owned + ghost :, :] + z[ghost : 2 * ghost]
    scale = scales[ghost:, :1]
    rows = scale * scale * (far_partial[...] + z[2 * ghost :])
    far_rows[...] = (sigma_one / filter_half) * (rows - filter_center * far_sent[...])


def first_own_kernel(far, near, partial, ham, column, s, base):
    owned = s.shape[0]
    z = partial[:owned, :] + halo_part(near[...], far[...], ham[:owned, :])
    base[...] = (sigma_one / filter_half) * (z * column[:, :1] - filter_center * s[...])


def far_rows_kernel(from_near, far_rows, far_is_near, scales, out):
    ghost, cols = far_rows.shape
    scale = scales[ghost:, :]
    added = (sigma_one / filter_half) * scale[:, :1] * scale[:, :1] * placed(from_near, far_is_near)
    out[...] = jnp.concatenate([far_rows[...] + added, scale], axis=1)


def near_sums_kernel(from_near, base, column, put_near, pick, out, near_rows):
    scale = column[:, :1]
    rows = base[...] + (sigma_one / filter_half) * scale * placed(from_near, put_near)
    out[...] = rows
    near_rows[...] = picked(rows * scale, pick[: near_rows.shape[0], :])


def near_rows_kernel(from_far, near_rows, near_is_far, scales, out):
    scale = scales[: out.shape[0], :1]
    added = (sigma_one / filter_half) * scale * scale * placed(from_far, near_is_far)
    out[...] = near_rows[...] + added


def far_sums_kernel(from_far, base, column, put_far, one):
    scale = (sigma_one / filter_half) * column[:, :1]
    one[...] = base[...] + scale * placed(from_far, put_far)


def second_sums_kernel(far, near, sent, partial, ham, to_near, to_far):
    ghost = near.shape[0]
    owned = partial.shape[0] - 2 * ghost
    z = partial[owned:, :] + halo_part(near[...], completed(far, sent), ham[owned:, :])
    to_near[...] = z[:ghost]
    to_far[...] = z[ghost:]


def second_own_kernel(far, near, sent, partial, ham, column, one, s, base):
    owned = s.shape[0]
    z = partial[:owned, :] + halo_part(near[...], completed(far, sent), ham[:owned, :])
    base[...] = (
        2.0 * sigma_two / filter_half * (z * column[:, :1] - filter_center * one[...])
        - sigma_one * sigma_two * s[...]
    )


def last_kernel(from_far, base, from_near, column, put_near, put_far, out):
    sums = placed(from_near, put_near) + placed(from_far, put_far)
    out[...] = base[...] + 2.0 * sigma_two / filter_half * column[:, :1] * sums


def order_kernel(owner, *refs):
    parts, (hi_out, lo_out) = refs[:-2], refs[-2:]
    here = lax.axis_index("dom")
    panel = lax.broadcasted_iota(jnp.int32, owner.shape, 1).astype(f32)
    for b, part in enumerate(parts):
        place = jnp.sum(jnp.where(owner[...] == (here ^ b), panel, 0.0)).astype(jnp.int32)
        hi, lo = split(part[...])
        hi_out[place] = hi
        lo_out[place] = lo


def left_side(rows):
    hi, lo = split(rows)
    return jnp.concatenate([hi, lo, hi], axis=1)


def rotated(left, hi_ref, lo_ref, distance):
    k = lax.axis_index("band") ^ distance
    rhi, rlo = hi_ref[k], lo_ref[k]
    return mm(left, jnp.concatenate([rhi, rhi, rlo], axis=0))


def left_kernel(own, one, two, out):
    for r, block in enumerate((own, one, two)):
        out[r] = left_side(block[...])


def longer_kernel(block, out):
    rows = block.shape[0]
    out[:rows, :] = block[...]
    out[rows:, :] = block[: out.shape[0] - rows, :]


def rotate_kernel(hi_ref, lo_ref, left, out):
    out[...] = sum(rotated(left[r], hi_ref, lo_ref, r) for r in range(left.shape[0]))


def rotate_last_kernel(hi_ref, lo_ref, total, three, column, pick, out, near_out, far_out):
    left = left_side(three[: total.shape[0], :])
    rows = total[...] + rotated(left, hi_ref, lo_ref, 3)
    out[...] = rows
    send_rows(rows * column[:, :1], pick, near_out, far_out)


def flip(count, bits):
    return [(i, i ^ bits) for i in range(count)]


def ordered_rotation(slots, owner, bands):
    rows, cols = slots[0].shape
    total = len(slots) * rows
    hi, lo = call(
        order_kernel,
        (shape(len(slots), rows, cols, dtype=bf16),) * 2,
        [owner[None, :], *slots],
        0,
    )
    return hi.reshape(bands, total // bands, cols), lo.reshape(bands, total // bands, cols)


def shards(states, inv_mass, cell_ham, cell_nodes, send_up, send_down, owner, rotation_store):
    owned, cols = states.shape
    ghost = send_up.shape[0]
    ext = owned + 2 * ghost
    doms, bands = lax.axis_size("dom"), lax.axis_size("band")
    m = inv_mass[None, :]
    up = send_up[None, :]
    dn = send_down[None, :]
    near_pairs = flip(doms, 1)
    far_pairs = [(i, (i - 1 if i % 2 == 0 else i + 1) % doms) for i in range(doms)]
    halo = shape(ghost, cols)
    block = shape(owned, cols)
    small = 4 * ghost * owned * cols * 3

    def to_pair(rows):
        return lax.ppermute(rows, "dom", near_pairs)

    def to_other(rows):
        return lax.ppermute(rows, "dom", far_pairs)

    ham_own, ham_halo = assemble(cell_nodes, cell_ham, ext, ghost)
    put = shape(owned, 2 * ghost, dtype=bf16)
    cross = shape(ghost, 2 * ghost, dtype=bf16)
    column, pick, put_near, put_far, far_is_near, near_is_far, scales = call(
        lists_kernel,
        (
            shape(owned, 128),
            shape(2 * ghost, 2 * owned, dtype=bf16),
            put,
            put,
            cross,
            cross,
            shape(2 * ghost, 128),
        ),
        [m, up, dn],
        owned * owned,
    )
    ham_send = call(
        send_ham_kernel, shape(3 * ghost, 6 * ghost, dtype=bf16), [ham_halo, pick], 0
    )
    band = lax.axis_index("band")
    own_columns = lax.dynamic_slice_in_dim(rotation_store, band * cols, cols, 1)
    one = lax.ppermute(states, "band", flip(4, 1))
    two = lax.ppermute(states, "band", flip(4, 2))
    paired = doms == 8 and rotation_store.shape[0] % 16 == 0
    parts = [own_columns]
    if paired:
        parts += [lax.ppermute(own_columns, "dom", flip(doms, b)) for b in (2, 4, 6)]
    one, two, ham_own = lax.optimization_barrier((one, two, ham_own))
    longer = call(longer_kernel, shape(owned + 1, cols), [two], 0)
    three = lax.ppermute(longer, "band", flip(4, 1))
    left = call(left_kernel, shape(3, owned, 3 * cols, dtype=bf16), [states, one, two], 0)
    left, *parts = lax.optimization_barrier((left, *parts))
    if paired:
        other = [lax.ppermute(part, "dom", near_pairs) for part in parts]
        slots = [part for pair in zip(parts, other) for part in pair]
        rotation = ordered_rotation(slots, owner, bands)
    else:
        columns = lax.all_gather(own_columns, "dom", axis=0, tiled=True)
        columns = columns.reshape(doms, -1, cols)[owner].reshape(bands, -1, cols)
        rotation = split(columns)
    work = 6 * owned * cols * cols
    total = call(rotate_kernel, block, [*rotation, left], 0)
    turned, to_near, to_far = call(
        rotate_last_kernel,
        (block, halo, halo),
        [*rotation, total, three, column, pick],
        work,
    )
    wide = shape(ext, cols)
    work = 6 * ext * ext * cols
    far, near = to_other(to_far), to_pair(to_near)
    partial, far_partial = call(
        first_partial_kernel, (wide, halo), [turned, column, ham_own, pick], work
    )
    to_near, sent, far_rows = call(
        first_sums_kernel,
        (halo, halo, halo),
        [far, near, partial, far_partial, to_far, ham_send, scales],
        0,
    )
    from_far, from_near = to_other(sent), to_pair(to_near)
    base = call(
        first_own_kernel, block, [far, near, partial, ham_halo, column, turned], 0
    )
    far = to_other(
        call(
            far_rows_kernel,
            shape(ghost, cols + 128),
            [from_near, far_rows, far_is_near, scales],
            0,
        )
    )
    base, near_rows = call(
        near_sums_kernel, (block, halo), [from_near, base, column, put_near, pick], 0
    )
    near = to_pair(
        call(near_rows_kernel, halo, [from_far, near_rows, near_is_far, scales], 0)
    )
    filtered = call(far_sums_kernel, block, [from_far, base, column, put_far], 0)
    partial = call(own_kernel, wide, [filtered, column, ham_own], work)
    to_near, to_far = call(
        second_sums_kernel, (halo, halo), [far, near, sent, partial, ham_halo], 0
    )
    from_far, from_near = to_other(to_far), to_pair(to_near)
    base = call(
        second_own_kernel,
        block,
        [far, near, sent, partial, ham_halo, column, filtered, turned],
        work,
    )
    operands = [from_far, base, from_near, column, put_near, put_far]
    return call(last_kernel, block, operands, small)


def solution(mesh):
    in_specs = (
        P("dom", "band"),
        P("dom"),
        P("dom", None, None),
        P("dom", None),
        P("dom"),
        P("dom"),
        P(),
        P("dom", None),
    )
    out_specs = P("dom", "band")
    return jax.shard_map(shards, mesh=mesh, in_specs=in_specs, out_specs=out_specs, check_vma=False)
```
